32 devices in a mesh: group: 2 (over x), tile: 4 (over y, core), orient: 4 (over z).
Axes of the slice: x: 2, y: 2, z: 4, core: 2. Of those that a mesh axis runs over, the one named last changes fastest.
Arguments:
- micrograph: float32 [768, 1024], P('group', 'tile'), parts along dimension 0, may hold values from -30 to 30
- templates: float32 [4, 4, 128, 128], P('orient', 'tile'), may hold values from 0 to 0.0107421875
- orient_ids: int32 [4, 4], P('orient', 'tile'), may hold values from 0 to 15, as said below
- log_weight: float32 [16], replicated, may hold values from -2 to 2
- ice_mask: int32 [32, 64], P('group', 'tile'), parts along dimension 0, may hold values 0 or 1
Outputs:
- score_map: float32 [512, 1024], P(('group', 'orient'), 'tile'), parts along dimension 0
The draws below stay inside these ranges and needn't reach their ends.
There are 2 independent parts, one for each index of `group`. The reference program is written for one: setup_inputs(seed, part) draws one part's arguments, and reference() takes and returns one part's arrays. A program takes and returns all parts, laid end to end along the dimension named above; an argument that names none is the same for every part. Nothing has to cross between parts.
Inputs may be any that keep to these rules, and one draw needn't show every extreme that they name: `orient_ids`: every slot holds a different orientation.
All inputs are finite; a program needn't handle non-finite values. No bound on the sum of `ice_mask` on one device may be relied on, other than what follows from the above.
Results may differ from the reference program's by a relative error of at most 0.00024.
Values sent between devices are 32-bit elements; how exact they have to be, the bound alone decides.
No kernel may reach another device: no remote copies, remote signals or barrier semaphores. Data moves between devices by JAX's collectives and lax.ppermute only.
A program may use at most 64 MiB of HBM per device.

```python
import jax
import jax.numpy as jnp
from jax import lax

TILE = 256
GUARD = 64
TPL = 128
MBLK = 16
EXT = 384
ORI_CYCLE = 4
ORI_BLOCKS = 4
ORIENTS = 16
WIDTH = 1024
N_TILE = 4


def bright_patches(third_key, fourth_key):
    row_starts = jax.random.randint(third_key, (3,), 0, min(TILE, EXT - TPL + 1))
    col_starts = jax.random.randint(fourth_key, (3,), 0, WIDTH - TPL + 1)
    row_grid = jnp.arange(EXT, dtype=jnp.int32)[:, None]
    col_grid = jnp.arange(WIDTH, dtype=jnp.int32)[None, :]
    strengths = jnp.array([120.0, 200.0, 300.0], jnp.float32) / (0.75 * TPL)
    bright = jnp.zeros((EXT, WIDTH), jnp.float32)
    for which in range(3):
        inside = (row_grid >= row_starts[which]) & (row_grid < row_starts[which] + TPL)
        inside = inside & (col_grid >= col_starts[which]) & (col_grid < col_starts[which] + TPL)
        bright = bright + jnp.where(inside, strengths[which], 0.0)
    return bright


def draw_micrograph(key, part):
    first_key, second_key, third_key, fourth_key = jax.random.split(key, 4)
    columns = jnp.arange(WIDTH, dtype=jnp.float32)
    ramp = 1.0 + 2.0 * columns[None, :] / max(WIDTH - 1, 1)
    rough = jax.random.uniform(second_key, (EXT, WIDTH), jnp.float32, 0.6, 1.6)
    bright = bright_patches(third_key, fourth_key)
    base = jnp.clip(jax.random.normal(first_key, (EXT, WIDTH), jnp.float32), -4.0, 4.0)
    field = base * ramp * rough + bright
    return jnp.clip(field, -30.0, 30.0)


def draw_templates(key, part):
    first_key, second_key = jax.random.split(key)
    scales = jax.random.uniform(first_key, (ORI_BLOCKS, ORI_CYCLE, 1, 1), jnp.float32, 0.9, 1.1)
    values = jax.random.uniform(second_key, (ORI_BLOCKS, ORI_CYCLE, TPL, TPL), jnp.float32, 0.0, 1.0)
    return scales * (0.25 + values) / TPL


def draw_orient_ids(key, part):
    order = jax.random.permutation(key, jnp.arange(ORIENTS, dtype=jnp.int32))
    return order.reshape(ORI_BLOCKS, ORI_CYCLE).astype(jnp.int32)


def set_ends(result, rng, least, top_value):
    place = [jax.random.randint(jax.random.fold_in(rng, axis), (), 0, length) for axis, length in enumerate(result.shape)]
    widest = result.shape.index(max(result.shape))
    neighbour = place[:widest] + [(place[widest] + 1) % result.shape[widest]] + place[widest + 1:]
    return result.at[tuple(place)].set(least).at[tuple(neighbour)].set(top_value)


def setup_inputs(seed: int = 0, part: int = 0) -> dict:
    seeds = jax.random.split(jax.random.key(seed), 6)
    part_keys = jax.random.split(jax.random.fold_in(seeds[5], part), 6)
    micrograph = draw_micrograph(jax.random.fold_in(jax.random.fold_in(seeds[5], part), 71), part)
    templates = draw_templates(jax.random.fold_in(seeds[5], 71), part)
    orient_ids = draw_orient_ids(jax.random.fold_in(seeds[5], 71), part)
    log_weight = jnp.clip(jax.random.uniform(seeds[3], (ORIENTS,), jnp.float32, -2.0, 2.0), -2.0, 2.0)
    ice_mask = set_ends((jax.random.randint(part_keys[4], (TILE // MBLK, WIDTH // MBLK), 0, 4) < 1).astype(jnp.int32), jax.random.fold_in(part_keys[4], 1), 0, 1)
    return dict(micrograph=micrograph, templates=templates, orient_ids=orient_ids, log_weight=log_weight, ice_mask=ice_mask)


def reference(micrograph, templates, orient_ids, log_weight, ice_mask):
    padded = jnp.pad(micrograph, ((0, 0), (GUARD, GUARD)))
    flat_templates = templates.reshape(ORIENTS, TPL, TPL)
    template_spec = jnp.fft.rfft2(flat_templates, s=(EXT, EXT))
    weights = log_weight[orient_ids.reshape(-1)]

    def one_tile(tile_index):
        window = lax.dynamic_slice_in_dim(padded, tile_index * TILE, EXT, 1)
        window_spec = jnp.fft.rfft2(window)
        correlation = jnp.fft.irfft2(window_spec[None] * jnp.conj(template_spec), s=(EXT, EXT))[:, :TILE, :TILE]
        scores = correlation + weights[:, None, None]
        return jax.scipy.special.logsumexp(scores, axis=0)
    per_tile = lax.map(one_tile, jnp.arange(N_TILE, dtype=jnp.int32))
    log_total = jnp.transpose(per_tile, (1, 0, 2)).reshape(TILE, WIDTH)
    blocks = jnp.repeat(jnp.repeat(ice_mask, MBLK, axis=0), MBLK, axis=1)
    unmasked = 1.0 - blocks.astype(jnp.float32)
    live_count = jnp.sum(unmasked)
    average = jnp.sum(unmasked * log_total) / live_count
    variance = jnp.sum(unmasked * (log_total - average) ** 2) / live_count
    return unmasked * (log_total - average) / jnp.sqrt(variance + 1e-05)
```

```python
import functools
import math

import jax
import jax.numpy as jnp
import ml_dtypes
import numpy as np
from jax import lax
from jax.experimental import pallas as pl
from jax.experimental.pallas import tpu as pltpu
from jax.sharding import PartitionSpec as P

GUARD = 64
MBLK = 16
LANES = 128
PACK = 8
CHUNK = 12

F32 = jnp.float32
BF16 = jnp.bfloat16
VMEM = pl.BlockSpec(memory_space=pltpu.VMEM)
SMEM = pl.BlockSpec(memory_space=pltpu.SMEM)


def params(mib):
    return pltpu.CompilerParams(vmem_limit_bytes=mib * 2**20)


def high_low(table):
    high = table.astype(np.float32).astype(ml_dtypes.bfloat16)
    low = (table - high.astype(np.float64)).astype(np.float32).astype(ml_dtypes.bfloat16)
    return high, low


def tables(side):
    span = 2 * side
    angles = np.outer(np.arange(span), 2.0 * math.pi * (np.arange(side) + 0.5) / span)
    basis = np.concatenate([np.cos(angles), np.sin(angles)], axis=1)
    high, low = high_low(basis)
    back_high, back_low = high_low(np.concatenate([np.cos(angles[:side]), -np.sin(angles[:side])], axis=1).T)
    return dict(
        image_cols=np.concatenate([high, high, low], axis=0),
        image_rows=np.concatenate([high.T, high.T, low.T], axis=1),
        patch_cols=np.concatenate([high[:side], high[:side], low[:side]], axis=0),
        patch_rows=np.concatenate([high[:side].T, high[:side].T, low[:side].T], axis=1),
        back_rows=np.concatenate([high[:side], high[:side], low[:side]], axis=1),
        back_cols=np.concatenate([back_high, back_high, back_low], axis=0),
    )


def split(x):
    high = x.astype(BF16)
    return high, (x - high.astype(F32)).astype(BF16)


def tripled(x, axis):
    high, low = split(x)
    return jnp.concatenate([high, low, high], axis=axis)


def product(left, right):
    return jnp.dot(left, right, preferred_element_type=F32)


def paired(quads, side):
    cc, cs = quads[:side, :side], quads[:side, side:]
    sc, ss = quads[side:, :side], quads[side:, side:]
    return cc - ss, sc + cs, cc + ss, sc - cs


def image_spectra(left_ref, own_ref, right_ref, cols_ref, rows_ref, spec_ref):
    image = jnp.concatenate([left_ref[...], own_ref[...], right_ref[...]], axis=1)
    side = spec_ref.shape[-1]
    span = 2 * side
    rows, cols = image.shape[0] // side - 1, image.shape[1] // side - 1
    scale = 2.0 / (span * span)
    for q in range(cols):
        half = product(tripled(image[:, q * side : q * side + span], 1), cols_ref[...])
        for p in range(rows):
            full = product(rows_ref[...], tripled(half[p * side : p * side + span], 0))
            for part, value in enumerate(paired(full, side)):
                spec_ref[p * cols + q, part] = value * scale


def correlate(spec_ref, patches, tabs, half_ref, patch_ref, score_ref):
    patch_cols, patch_rows, back_rows, back_cols = tabs
    side = spec_ref.shape[-1]
    count = len(patches)
    cols = score_ref.shape[2] // side
    for first in range(0, count, 4):
        group = patches[first : first + 4]
        half = product(tripled(jnp.concatenate(group, axis=0), 1), patch_cols[...])
        for i in range(len(group)):
            high, low = split(half[i * side : (i + 1) * side])
            half_ref[first + i, 0:side] = high
            half_ref[first + i, side : 2 * side] = low
            half_ref[first + i, 2 * side : 3 * side] = high

    def finish_patch(n, carry):
        for part, value in enumerate(paired(product(patch_rows[...], half_ref[n]), side)):
            patch_ref[n, part] = value
        return carry

    def score(n, carry):
        tr, tu, sr, si = (patch_ref[n, part] for part in range(4))
        for block in range(spec_ref.shape[0]):
            p, q = divmod(block, cols)
            ir, iu, jr, ji = (spec_ref[block, part] for part in range(4))
            a, b = ir * tr + iu * tu, ir * tu - iu * tr
            c, d = jr * sr + ji * si, ji * sr - jr * si
            top = jnp.concatenate([a + c, b + d], axis=1)
            low = jnp.concatenate([d - b, a - c], axis=1)
            lines = product(back_rows[...], tripled(jnp.concatenate([top, low], axis=0), 0))
            score_ref[n, p * side : (p + 1) * side, q * side : (q + 1) * side] = product(
                tripled(lines, 1), back_cols[...]
            )
        return carry

    unroll = max(u for u in (1, 2, 3, 4) if count % u == 0)
    lax.fori_loop(0, count, finish_patch, 0, unroll=unroll)
    lax.fori_loop(0, count, score, 0, unroll=unroll)


STRIP = 16


def fold(score_ref, weights, state, out):
    def strip(r, carry):
        rows = pl.ds(pl.multiple_of(r * STRIP, STRIP), STRIP)
        values = [score_ref[n, rows, :] + weight for n, weight in enumerate(weights)]
        top = values[0]
        for value in values[1:]:
            top = jnp.maximum(top, value)
        if state is not None:
            old_top, old_sum = state[0][rows, :], state[1][rows, :]
            top = jnp.maximum(top, old_top)
        total = jnp.exp(values[0] - top)
        for value in values[1:]:
            total = total + jnp.exp(value - top)
        if state is not None:
            total = total + old_sum * jnp.exp(old_top - top)
        out(rows, top, total)
        return carry

    lax.fori_loop(0, score_ref.shape[1] // STRIP, strip, 0)


def unpack(refs, side):
    patches, weights = [], []
    for ref in refs:
        if len(ref.shape) == 2:
            patches.append(ref[0:side, :])
            weights.append(ref[side : side + 1, 0:1])
        else:
            for i in range(ref.shape[0]):
                patches.append(ref[i, 0:side, :])
                weights.append(ref[i, side : side + 1, 0:1])
    return patches, weights


def first_kernel(n_in, *refs):
    left, own, right, image_cols, image_rows = refs[:5]
    tabs, packs = refs[5:9], refs[9 : 9 + n_in]
    spec_ref, top_ref, sum_ref, half_ref, patch_ref, score_ref = refs[9 + n_in :]
    image_spectra(left, own, right, image_cols, image_rows, spec_ref)
    patches, weights = unpack(packs, spec_ref.shape[-1])
    correlate(spec_ref, patches, tabs, half_ref, patch_ref, score_ref)

    def out(rows, top, total):
        top_ref[rows, :] = top
        sum_ref[rows, :] = total

    fold(score_ref, weights, None, out)


def next_kernel(n_in, *refs):
    spec_ref, old_top, old_sum = refs[:3]
    tabs, packs = refs[3:7], refs[7 : 7 + n_in]
    top_ref, sum_ref, half_ref, patch_ref, score_ref = refs[7 + n_in :]
    patches, weights = unpack(packs, spec_ref.shape[-1])
    correlate(spec_ref, patches, tabs, half_ref, patch_ref, score_ref)

    def out(rows, top, total):
        top_ref[rows, :] = top
        sum_ref[rows, :] = total

    fold(score_ref, weights, (old_top, old_sum), out)


def unmasked_pixels(mask_ref):
    blocks = (1.0 - mask_ref[...].astype(F32)).astype(BF16)
    rows, cols = blocks.shape

    def spread(count, axis):
        shape = (count * MBLK, count) if axis == 0 else (count, count * MBLK)
        pixel = lax.broadcasted_iota(jnp.int32, shape, axis)
        block = lax.broadcasted_iota(jnp.int32, shape, 1 - axis)
        return ((pixel >= block * MBLK) & (pixel < (block + 1) * MBLK)).astype(F32).astype(BF16)

    return product(product(spread(rows, 0), blocks).astype(BF16), spread(cols, 1))


def last_kernel(n_in, share, *refs):
    place_ref, mask_ref, spec_ref, old_top, old_sum = refs[:5]
    tabs, packs = refs[5:9], refs[9 : 9 + n_in]
    part_ref, open_ref, stat_ref, half_ref, patch_ref, score_ref, log_ref, pixel_ref = refs[9 + n_in :]
    patches, weights = unpack(packs, spec_ref.shape[-1])
    correlate(spec_ref, patches, tabs, half_ref, patch_ref, score_ref)

    def out(rows, top, total):
        log_ref[rows, :] = top + jnp.log(total)

    fold(score_ref, weights, (old_top, old_sum), out)
    pixels = unmasked_pixels(mask_ref)
    pixel_ref[...] = pixels
    values = log_ref[...]
    count = jnp.sum(pixels)
    total = jnp.sum(pixels * values)
    deviation = values - total / jnp.maximum(count, 1.0)
    squares = jnp.sum(pixels * deviation * deviation)
    lane = lax.broadcasted_iota(jnp.int32, stat_ref.shape, 1)
    stat_ref[...] = jnp.where(lane == 0, count, jnp.where(lane == 1, total, squares))
    own = pl.ds(pl.multiple_of(place_ref[0] * share, share), share)
    part_ref[...] = log_ref[own, :]
    open_ref[...] = pixel_ref[own, :]


def norm_kernel(part_ref, open_ref, *refs):
    stats, out_ref = refs[:-1], refs[-1]
    counts = [ref[:, 0:1] for ref in stats]
    totals = [ref[:, 1:2] for ref in stats]
    count, total = sum(counts), sum(totals)
    average = total / count
    squares = 0.0
    for ref, n, s in zip(stats, counts, totals):
        apart = s / jnp.maximum(n, 1.0) - average
        squares = squares + ref[:, 2:3] + n * apart * apart
    scale = 1.0 / jnp.sqrt(squares / count + 1e-05)
    out_ref[...] = open_ref[...] * (part_ref[...] - average[0:1]) * scale[0:1]


def peer(x, axis, step):
    n = lax.axis_size(axis)
    if n & (n - 1):
        pairs = [(i, (i + step) % n) for i in range(n)]
    else:
        pairs = [(i, i ^ step) for i in range(n)]
    return lax.ppermute(x, axis, pairs)


def swap(x, axis):
    return lax.ppermute(x, axis, [(i, i ^ 1) for i in range(lax.axis_size(axis))])


def halo(own, axis):
    n = lax.axis_size(axis)
    up = [(i, i + 1) for i in range(n - 1)]
    left = lax.ppermute(own[:, own.shape[1] - GUARD :], axis, up)
    right = lax.ppermute(own[:, :GUARD], axis, [(j, i) for i, j in up])
    return left, right


def chunks(arrays):
    groups, held = [[]], 0
    for x in arrays:
        if held + x.shape[0] > CHUNK and groups[-1]:
            groups.append([])
            held = 0
        groups[-1].append(x)
        held += x.shape[0]
    return groups


def body(micrograph, templates, orient_ids, log_weight, ice_mask):
    side = templates.shape[2]
    tile = micrograph.shape[1]
    blocks = (tile // side) ** 2
    tab = {name: jnp.asarray(value) for name, value in tables(side).items()}
    tabs = [tab["patch_cols"], tab["patch_rows"], tab["back_rows"], tab["back_cols"]]
    place = lax.axis_index("orient").astype(jnp.int32).reshape(1)

    catalog = lax.broadcasted_iota(jnp.int32, log_weight.shape, 0)
    weight = jnp.sum(jnp.where(catalog == orient_ids[0, 0], log_weight, 0.0))
    pack = jnp.concatenate([templates[0, 0], jnp.full((PACK, side), weight, F32)], axis=0)

    n_tile, n_orient = lax.axis_size("tile"), lax.axis_size("orient")
    far = [peer(pack, "orient", k) for k in range(1, n_orient)]
    left, right = halo(micrograph, "tile")
    even = n_tile % 2 == 0
    steps = range(2, n_tile, 2) if even else range(1, n_tile)
    near = [peer(pack, "tile", k) for k in steps]
    mine = [pack, *near]
    if even:
        mine += [swap(x, "tile") for x in mine]
    rest = [jnp.stack(far)] if far else []
    held = rest + [peer(x, "tile", k) for x in rest for k in steps]
    groups = [[x] for x in held]
    if even:
        groups += chunks([swap(x, "tile") for x in held])

    spectra = jax.ShapeDtypeStruct((blocks, 4, side, side), F32)
    plane = jax.ShapeDtypeStruct((tile, tile), F32)

    def scratch(n):
        return [
            pltpu.VMEM((n, 3 * side, 2 * side), BF16),
            pltpu.VMEM((n, 4, side, side), F32),
            pltpu.VMEM((n, tile, tile), F32),
        ]

    def size(group):
        return sum(x.shape[0] if x.ndim == 3 else 1 for x in group)

    spec, top, total = pl.pallas_call(
        functools.partial(first_kernel, len(mine)),
        out_shape=(spectra, plane, plane),
        in_specs=[VMEM] * (9 + len(mine)),
        out_specs=(VMEM,) * 3,
        scratch_shapes=scratch(len(mine)),
        compiler_params=params(40),
        name="own_block",
    )(left, micrograph, right, tab["image_cols"], tab["image_rows"], *tabs, *mine)
    for group in groups[:-1]:
        top, total = pl.pallas_call(
            functools.partial(next_kernel, len(group)),
            out_shape=(plane, plane),
            in_specs=[VMEM] * (7 + len(group)),
            out_specs=(VMEM,) * 2,
            scratch_shapes=scratch(size(group)),
            compiler_params=params(40),
            name="next_block",
        )(spec, top, total, *tabs, *group)
    group = groups[-1]
    share = tile // n_orient
    part = jax.ShapeDtypeStruct((share, tile), F32)
    part, opened, stat = pl.pallas_call(
        functools.partial(last_kernel, len(group), share),
        out_shape=(part, part, jax.ShapeDtypeStruct((8, LANES), F32)),
        in_specs=[SMEM] + [VMEM] * (8 + len(group)),
        out_specs=(VMEM,) * 3,
        scratch_shapes=scratch(size(group)) + [pltpu.VMEM((tile, tile), F32)] * 2,
        compiler_params=params(40),
        name="last_block",
    )(place, ice_mask, spec, top, total, *tabs, *group)
    stats = [stat] + [peer(stat, "tile", k) for k in range(1, n_tile)]
    return pl.pallas_call(
        norm_kernel,
        out_shape=jax.ShapeDtypeStruct((share, tile), F32),
        in_specs=[VMEM] * (2 + len(stats)),
        out_specs=VMEM,
        name="normalise",
    )(part, opened, *stats)


def solution(mesh):
    return jax.shard_map(
        body,
        mesh=mesh,
        in_specs=(
            P("group", "tile"),
            P("orient", "tile", None, None),
            P("orient", "tile"),
            P(),
            P("group", "tile"),
        ),
        out_specs=P(("group", "orient"), "tile"),
        check_vma=False,
    )
```

```python
import functools
import math

import jax
import jax.numpy as jnp
import ml_dtypes
import numpy as np
from jax import lax
from jax.experimental import pallas as pl
from jax.experimental.pallas import tpu as pltpu
from jax.sharding import PartitionSpec as P

GUARD = 64
MBLK = 16
LANES = 128
PACK = 8
BARRIER = True

F32 = jnp.float32
BF16 = jnp.bfloat16
VMEM = pl.BlockSpec(memory_space=pltpu.VMEM)
SMEM = pl.BlockSpec(memory_space=pltpu.SMEM)


def params(mib):
    return pltpu.CompilerParams(vmem_limit_bytes=mib * 2**20)


def high_low(table):
    high = table.astype(np.float32).astype(ml_dtypes.bfloat16)
    low = (table - high.astype(np.float64)).astype(np.float32).astype(ml_dtypes.bfloat16)
    return high, low


def tables(side):
    span = 2 * side
    angles = np.outer(np.arange(span), 2.0 * math.pi * (np.arange(side) + 0.5) / span)
    high, low = high_low(np.concatenate([np.cos(angles), np.sin(angles)], axis=1))
    return np.concatenate([high, low, high.T, low.T], axis=0)


def tall(tab_ref, part, count):
    span = tab_ref.shape[1]
    high = tab_ref[part * span : part * span + count, :]
    low = tab_ref[(part + 1) * span : (part + 1) * span + count, :]
    return jnp.concatenate([high, high, low], axis=0)


def wide(tab_ref, part, rows, cols):
    span = tab_ref.shape[1]
    high = tab_ref[part * span : part * span + rows, 0:cols]
    low = tab_ref[(part + 1) * span : (part + 1) * span + rows, 0:cols]
    return jnp.concatenate([high, high, low], axis=1)


def back_cols(tab_ref, side):
    span = tab_ref.shape[1]
    high = tab_ref[2 * span : 3 * span, 0:side]
    low = tab_ref[3 * span : 4 * span, 0:side]
    return jnp.concatenate([high, high, low], axis=0)


def split(x):
    high = x.astype(BF16)
    return high, (x - high.astype(F32)).astype(BF16)


def tripled(x, axis):
    high, low = split(x)
    return jnp.concatenate([high, low, high], axis=axis)


def product(left, right):
    return jnp.dot(left, right, preferred_element_type=F32)


def paired(quads, side):
    cc, cs = quads[:side, :side], quads[:side, side:]
    sc, ss = quads[side:, :side], quads[side:, side:]
    return cc - ss, sc + cs, cc + ss, sc - cs


def image_spectra(odd_ref, inner_ref, own_ref, outer_ref, tab_ref, spec_ref):
    odd = odd_ref[0] == 1
    inner, outer = inner_ref[...], outer_ref[...]
    left, right = jnp.where(odd, inner, outer), jnp.where(odd, outer, inner)
    image = jnp.concatenate([left, own_ref[...], right], axis=1)
    side = spec_ref.shape[-1]
    span = 2 * side
    rows, cols = image.shape[0] // side - 1, image.shape[1] // side - 1
    scale = 2.0 / (span * span)
    cols_table, rows_table = tall(tab_ref, 0, span), wide(tab_ref, 2, span, span)
    for q in range(cols):
        half = product(tripled(image[:, q * side : q * side + span], 1), cols_table)
        for p in range(rows):
            full = product(rows_table, tripled(half[p * side : p * side + span], 0))
            for part, value in enumerate(paired(full, side)):
                spec_ref[p * cols + q, part] = value * scale


def correlate(spec_ref, patches, tab_ref, half_ref, patch_ref, score_ref):
    side = spec_ref.shape[-1]
    span = 2 * side
    patch_cols, patch_rows = tall(tab_ref, 0, side), wide(tab_ref, 2, span, side)
    rows_table, cols_table = wide(tab_ref, 0, side, span), back_cols(tab_ref, side)
    count = len(patches)
    cols = score_ref.shape[2] // side
    for first in range(0, count, 4):
        group = patches[first : first + 4]
        half = product(tripled(jnp.concatenate(group, axis=0), 1), patch_cols)
        for i in range(len(group)):
            high, low = split(half[i * side : (i + 1) * side])
            half_ref[first + i, 0:side] = high
            half_ref[first + i, side : 2 * side] = low
            half_ref[first + i, 2 * side : 3 * side] = high

    def finish_patch(n, carry):
        for part, value in enumerate(paired(product(patch_rows, half_ref[n]), side)):
            patch_ref[n, part] = value
        return carry

    def score(n, carry):
        tr, tu, sr, si = (patch_ref[n, part] for part in range(4))
        for block in range(spec_ref.shape[0]):
            p, q = divmod(block, cols)
            ir, iu, jr, ji = (spec_ref[block, part] for part in range(4))
            a, b = ir * tr + iu * tu, iu * tr - ir * tu
            c, e = jr * sr + ji * si, jr * si - ji * sr
            top = jnp.concatenate([a + c, e + b], axis=1)
            low = jnp.concatenate([b - e, c - a], axis=1)
            lines = product(rows_table, tripled(jnp.concatenate([top, low], axis=0), 0))
            score_ref[n, p * side : (p + 1) * side, q * side : (q + 1) * side] = product(
                tripled(lines, 1), cols_table
            )
        return carry

    unroll = max(u for u in (1, 2, 3, 4) if count % u == 0)
    lax.fori_loop(0, count, finish_patch, 0, unroll=unroll)
    lax.fori_loop(0, count, score, 0, unroll=unroll)


STRIP = 64


def fold(score_ref, weights, state, out):
    def strip(r, carry):
        rows = pl.ds(pl.multiple_of(r * STRIP, STRIP), STRIP)
        values = [score_ref[n, rows, :] + weight for n, weight in enumerate(weights)]
        top = values[0]
        for value in values[1:]:
            top = jnp.maximum(top, value)
        if state:
            old_top, old_sum = state[0][rows, :], state[1][rows, :]
            top = jnp.maximum(top, old_top)
        total = jnp.exp(values[0] - top)
        for value in values[1:]:
            total = total + jnp.exp(value - top)
        if state:
            total = total + old_sum * jnp.exp(old_top - top)
        out(rows, top, total)
        return carry

    lax.fori_loop(0, score_ref.shape[1] // STRIP, strip, 0, unroll=True)


def unpack(refs, side):
    patches, weights = [], []
    for ref in refs:
        places = [()] if len(ref.shape) == 2 else [(i,) for i in range(ref.shape[0])]
        for place in places:
            patches.append(ref[place + (slice(0, side), slice(None))])
            weights.append(ref[place + (slice(side, side + 1), slice(0, 1))])
    return patches, weights


def first_kernel(n_in, *refs):
    packs = refs[5 : 5 + n_in]
    spec_ref, top_ref, sum_ref, half_ref, patch_ref, score_ref = refs[5 + n_in :]
    image_spectra(*refs[:5], spec_ref)
    score_kernel(packs, spec_ref, (), refs[4], top_ref, sum_ref, half_ref, patch_ref, score_ref)


def score_kernel(packs, spec_ref, state, tab_ref, top_ref, sum_ref, half_ref, patch_ref, score_ref):
    patches, weights = unpack(packs, spec_ref.shape[-1])
    correlate(spec_ref, patches, tab_ref, half_ref, patch_ref, score_ref)

    def out(rows, top, total):
        top_ref[rows, :] = top
        sum_ref[rows, :] = total

    fold(score_ref, weights, state, out)


def next_kernel(n_state, n_in, *refs):
    spec_ref, state, tab_ref = refs[0], refs[1 : 1 + n_state], refs[1 + n_state]
    score_kernel(refs[2 + n_state : 2 + n_state + n_in], spec_ref, state, tab_ref, *refs[2 + n_state + n_in :])


def unmasked_pixels(mask_ref):
    blocks = (1.0 - mask_ref[...].astype(F32)).astype(BF16)
    rows, cols = blocks.shape

    def spread(count, axis):
        shape = (count * MBLK, count) if axis == 0 else (count, count * MBLK)
        pixel = lax.broadcasted_iota(jnp.int32, shape, axis)
        block = lax.broadcasted_iota(jnp.int32, shape, 1 - axis)
        return ((pixel >= block * MBLK) & (pixel < (block + 1) * MBLK)).astype(F32).astype(BF16)

    return product(product(spread(rows, 0), blocks).astype(BF16), spread(cols, 1))


def last_kernel(n_in, share, *refs):
    place_ref, mask_ref, spec_ref, old_top, old_sum, tab_ref = refs[:6]
    packs = refs[6 : 6 + n_in]
    part_ref, open_ref, stat_ref, half_ref, patch_ref, score_ref, log_ref, pixel_ref = refs[6 + n_in :]
    patches, weights = unpack(packs, spec_ref.shape[-1])
    correlate(spec_ref, patches, tab_ref, half_ref, patch_ref, score_ref)

    def out(rows, top, total):
        log_ref[rows, :] = top + jnp.log(total)

    fold(score_ref, weights, (old_top, old_sum), out)
    pixels = unmasked_pixels(mask_ref)
    pixel_ref[...] = pixels
    values = log_ref[...]
    count = jnp.sum(pixels)
    total = jnp.sum(pixels * values)
    deviation = values - total / jnp.maximum(count, 1.0)
    squares = jnp.sum(pixels * deviation * deviation)
    lane = lax.broadcasted_iota(jnp.int32, stat_ref.shape, 1)
    stat_ref[...] = jnp.where(lane == 0, count, jnp.where(lane == 1, total, squares))
    own = pl.ds(pl.multiple_of(place_ref[0] * share, share), share)
    part_ref[...] = log_ref[own, :]
    open_ref[...] = pixel_ref[own, :]


def norm_kernel(part_ref, open_ref, *refs):
    stats, out_ref = refs[:-1], refs[-1]
    counts = [ref[:, 0:1] for ref in stats]
    totals = [ref[:, 1:2] for ref in stats]
    count, total = sum(counts), sum(totals)
    average = total / count
    squares = 0.0
    for ref, n, s in zip(stats, counts, totals):
        apart = s / jnp.maximum(n, 1.0) - average
        squares = squares + ref[:, 2:3] + n * apart * apart
    scale = 1.0 / jnp.sqrt(squares / count + 1e-05)
    out_ref[...] = open_ref[...] * (part_ref[...] - average[0:1]) * scale[0:1]


def peer(x, axis, step):
    n = lax.axis_size(axis)
    if n & (n - 1):
        pairs = [(i, (i + step) % n) for i in range(n)]
    else:
        pairs = [(i, i ^ step) for i in range(n)]
    return lax.ppermute(x, axis, pairs)


def swap(x, axis):
    return lax.ppermute(x, axis, [(i, i ^ 1) for i in range(lax.axis_size(axis))])


def halo(own, axis):
    n = lax.axis_size(axis)
    odd = lax.axis_index(axis) % 2 == 1
    first, last = own[:, :GUARD], own[:, own.shape[1] - GUARD :]

    def exchange(edge, start):
        pairs = [(i, i + 1) for i in range(start, n - 1, 2)]
        return lax.ppermute(edge, axis, pairs + [(j, i) for i, j in pairs])

    return exchange(jnp.where(odd, first, last), 0), exchange(jnp.where(odd, last, first), 1)


def pack_kernel(ids_ref, weight_ref, patch_ref, pack_ref):
    side = patch_ref.shape[0]
    pack_ref[0:side, :] = patch_ref[...]
    catalog = lax.broadcasted_iota(jnp.int32, weight_ref.shape, 1)
    weight = jnp.sum(jnp.where(catalog == ids_ref[...], weight_ref[...], 0.0), axis=1, keepdims=True)
    pack_ref[side:, :] = jnp.broadcast_to(weight, (PACK, side))


def cost(micros):
    return pl.CostEstimate(flops=int(micros * 1e9), bytes_accessed=0, transcendentals=0)


def body(micrograph, templates, orient_ids, log_weight, ice_mask):
    side = templates.shape[2]
    tile = micrograph.shape[1]
    blocks = (tile // side) ** 2
    tab = jnp.asarray(tables(side))
    place = lax.axis_index("orient").astype(jnp.int32).reshape(1)
    pack = pl.pallas_call(
        pack_kernel,
        out_shape=jax.ShapeDtypeStruct((side + PACK, side), F32),
        in_specs=[VMEM] * 3,
        out_specs=VMEM,
        compiler_params=params(60),
        cost_estimate=cost(1),
        name="pack_weight",
    )(orient_ids, log_weight.reshape(1, -1), templates.reshape(side, side))

    n_tile, n_orient = lax.axis_size("tile"), lax.axis_size("orient")
    far = [peer(pack, "orient", k) for k in range(1, n_orient)]
    inner, outer = halo(micrograph, "tile")
    even = n_tile % 2 == 0
    steps = range(2, n_tile, 2) if even else range(1, n_tile)
    mine = [pack] + [peer(pack, "tile", k) for k in steps]
    if even:
        mine += [swap(x, "tile") for x in mine]
    odd = (lax.axis_index("tile") % 2).astype(jnp.int32).reshape(1)

    plane = jax.ShapeDtypeStruct((tile, tile), F32)

    def scratch(n):
        return [
            pltpu.VMEM((n, 3 * side, 2 * side), BF16),
            pltpu.VMEM((n, 4, side, side), F32),
            pltpu.VMEM((n, tile, tile), F32),
        ]

    def size(group):
        return sum(x.shape[0] if x.ndim == 3 else 1 for x in group)

    spec, *state = pl.pallas_call(
        functools.partial(first_kernel, len(mine)),
        out_shape=(jax.ShapeDtypeStruct((blocks, 4, side, side), F32), plane, plane),
        in_specs=[SMEM] + [VMEM] * (4 + len(mine)),
        out_specs=(VMEM,) * 3,
        scratch_shapes=scratch(len(mine)),
        compiler_params=params(24),
        cost_estimate=cost(5),
        name="own_block",
    )(odd, inner, micrograph, outer, tab, *mine)

    def score(state, arrays):
        return pl.pallas_call(
            functools.partial(next_kernel, len(state), len(arrays)),
            out_shape=(plane, plane),
            in_specs=[VMEM] * (2 + len(state) + len(arrays)),
            out_specs=(VMEM,) * 2,
            scratch_shapes=scratch(size(arrays)),
            compiler_params=params(24),
            cost_estimate=cost(size(arrays)),
            name="next_block",
        )(spec, *state, tab, *arrays)

    if BARRIER:
        far, state = lax.optimization_barrier((far, state))
    held = jnp.stack(far)
    near = [peer(held, "tile", k) for k in steps]
    state = score(state, [held, swap(held, "tile")] if even else [held])
    if near:
        near, state = lax.optimization_barrier((near, state))
    groups = [[x, swap(x, "tile")] if even else [x] for x in near]
    for group in groups[:-1]:
        state = score(state, group)
    top, total = state
    group = groups[-1]
    share = tile // n_orient
    part = jax.ShapeDtypeStruct((share, tile), F32)
    part, opened, stat = pl.pallas_call(
        functools.partial(last_kernel, len(group), share),
        out_shape=(part, part, jax.ShapeDtypeStruct((8, LANES), F32)),
        in_specs=[SMEM] + [VMEM] * (5 + len(group)),
        out_specs=(VMEM,) * 3,
        scratch_shapes=scratch(size(group)) + [pltpu.VMEM((tile, tile), F32)] * 2,
        compiler_params=params(24),
        cost_estimate=cost(size(group)),
        name="last_block",
    )(place, ice_mask, spec, top, total, tab, *group)
    stats = [stat] + [peer(stat, "tile", k) for k in range(1, n_tile)]
    return pl.pallas_call(
        norm_kernel,
        out_shape=jax.ShapeDtypeStruct((share, tile), F32),
        in_specs=[VMEM] * (2 + len(stats)),
        out_specs=VMEM,
        compiler_params=params(4),
        cost_estimate=cost(1),
        name="normalise",
    )(part, opened, *stats)


def solution(mesh):
    return jax.shard_map(
        body,
        mesh=mesh,
        in_specs=(
            P("group", "tile"),
            P("orient", "tile", None, None),
            P("orient", "tile"),
            P(),
            P("group", "tile"),
        ),
        out_specs=P(("group", "orient"), "tile"),
        check_vma=False,
    )
```

```python
import functools
import math

import jax
import jax.numpy as jnp
import ml_dtypes
import numpy as np
from jax import lax
from jax.experimental import pallas as pl
from jax.experimental.pallas import tpu as pltpu
from jax.sharding import PartitionSpec as P

GUARD = 64
MBLK = 16
LANES = 128
PACK = 8
CHUNK = 8
COST = 0.1

F32 = jnp.float32
BF16 = jnp.bfloat16
VMEM = pl.BlockSpec(memory_space=pltpu.VMEM)
SMEM = pl.BlockSpec(memory_space=pltpu.SMEM)


def params(mib):
    return pltpu.CompilerParams(vmem_limit_bytes=mib * 2**20)


def high_low(table):
    high = table.astype(np.float32).astype(ml_dtypes.bfloat16)
    low = (table - high.astype(np.float64)).astype(np.float32).astype(ml_dtypes.bfloat16)
    return high, low


def tables(side):
    span = 2 * side
    turn = 2.0 * math.pi * (np.arange(side) + 0.5) / span
    angles = np.outer(np.arange(span), turn)
    high, low = high_low(np.concatenate([np.cos(angles), np.sin(angles)], axis=1))
    middle = np.outer(np.arange(span) - (side - 1) / 2, turn)
    middle_high, middle_low = high_low(np.concatenate([np.cos(middle), np.sin(middle)], axis=1).T)
    away = np.outer(np.arange(side // 2) + 0.5, turn)
    ends = []
    for wave in (np.cos(away), np.sin(away)):
        wave_high, wave_low = high_low(wave)
        ends += [np.concatenate([wave_high, wave_high], axis=1), np.concatenate([wave_low, wave_low], axis=1)]
    return np.concatenate([high, low, high.T, low.T, *ends, middle_high, middle_low], axis=0)


def tall(tab_ref, count):
    span = tab_ref.shape[1]
    high, low = tab_ref[0:count, :], tab_ref[span : span + count, :]
    return jnp.concatenate([high, high, low], axis=0)


def wide(high, low):
    return jnp.concatenate([high, high, low], axis=1)


def back_cols(tab_ref, side):
    span = tab_ref.shape[1]
    both = jnp.concatenate([tab_ref[2 * span : 3 * span, 0:side], tab_ref[3 * span : 4 * span, 0:side]], axis=1)
    return jnp.concatenate([both, both], axis=0)


def split(x):
    high = x.astype(BF16)
    return high, (x - high.astype(F32)).astype(BF16)


def tripled(x, axis):
    high, low = split(x)
    return jnp.concatenate([high, low, high], axis=axis)


def doubled(x, axis):
    return jnp.concatenate(split(x), axis=axis)


def halves(x, axis):
    half = x.shape[axis] // 2
    return x[:half] + x[half:] if axis == 0 else x[:, :half] + x[:, half:]


def product(left, right):
    return jnp.dot(left, right, preferred_element_type=F32)


def paired(quads, side):
    cc, cs = quads[:side, :side], quads[:side, side:]
    sc, ss = quads[side:, :side], quads[side:, side:]
    return cc - ss, sc + cs, cc + ss, sc - cs


def image_spectra(spot_ref, inner_ref, own_ref, outer_ref, tab_ref, spec_ref):
    odd = spot_ref[0] % 2 == 1

    def edge(ref):
        lines = ref[...]
        return jnp.concatenate([lines[:, :GUARD], lines[:, GUARD:]], axis=0)

    inner, outer = edge(inner_ref), edge(outer_ref)
    left, right = jnp.where(odd, inner, outer), jnp.where(odd, outer, inner)
    image = jnp.concatenate([left, own_ref[...], right], axis=1)
    side = spec_ref.shape[-1]
    span = 2 * side
    rows, cols = image.shape[0] // side - 1, image.shape[1] // side - 1
    scale = 2.0 / (span * span)
    cols_table, rows_table = tall(tab_ref, span), wide(tab_ref[5 * span : 6 * span, :], tab_ref[6 * span :, :])
    for q in range(cols):
        half = product(tripled(image[:, q * side : q * side + span], 1), cols_table)
        for p in range(rows):
            full = product(rows_table, tripled(half[p * side : p * side + span], 0))
            for part, value in enumerate(paired(full, side)):
                spec_ref[p * cols + q, part] = value * scale


def transform(patches, tab_ref, half_ref, patch_ref):
    side = patch_ref.shape[-1]
    span = 2 * side
    patch_cols = tall(tab_ref, side)
    patch_rows = wide(tab_ref[2 * span : 3 * span, 0:side], tab_ref[3 * span : 4 * span, 0:side])
    for first in range(0, len(patches), 4):
        group = patches[first : first + 4]
        half = product(tripled(jnp.concatenate(group, axis=0), 1), patch_cols)
        for i in range(len(group)):
            high, low = split(half[i * side : (i + 1) * side])
            half_ref[first + i, 0:side] = high
            half_ref[first + i, side : 2 * side] = low
            half_ref[first + i, 2 * side : 3 * side] = high

    def finish(n, carry):
        for part, value in enumerate(paired(product(patch_rows, half_ref[n]), side)):
            patch_ref[n, part] = value
        return carry

    lax.fori_loop(0, len(patches), finish, 0, unroll=steps_at_once(len(patches), 8))


def steps_at_once(count, most):
    return max(u for u in range(1, most + 1) if count % u == 0)


def correlate(spec_ref, tab_ref, patch_ref, strips, score_ref):
    side = spec_ref.shape[-1]
    span = 2 * side
    cols = score_ref.shape[2] // side
    even_rows, odd_rows = tab_ref[4 * span : 4 * span + side, :], tab_ref[4 * span + side : 5 * span, :]
    cols_table = back_cols(tab_ref, side)

    def score(n, carry):
        tr, tu, sr, si = (patch_ref[n, part] for part in range(4))
        for p, strip in enumerate(strips):
            for q in range(cols):
                ir, iu, jr, ji = (spec_ref[strip * cols + q, part] for part in range(4))
                a, b = ir * tr + iu * tu, iu * tr - ir * tu
                c, e = jr * sr + ji * si, jr * si - ji * sr
                top = jnp.concatenate([a + c, e + b], axis=1)
                low = jnp.concatenate([b - e, c - a], axis=1)
                even = halves(product(even_rows, doubled(top, 0)), 0)
                odd = halves(product(odd_rows, doubled(low, 0)), 0)
                lines = jnp.concatenate([even + odd, even - odd], axis=0)
                score_ref[n, p * side : (p + 1) * side, q * side : (q + 1) * side] = halves(
                    product(doubled(lines, 1), cols_table), 1
                )
        return carry

    count = score_ref.shape[0]
    lax.fori_loop(0, count, score, 0, unroll=steps_at_once(count, 24 // (cols * len(strips))))


STRIP = 64


def fold(score_ref, weights, state, start, out):
    def strip(r, carry):
        first = pl.multiple_of(r * STRIP, STRIP)
        rows, whole = pl.ds(first, STRIP), pl.ds(first + start, STRIP)
        values = [score_ref[n, rows, :] + weight for n, weight in enumerate(weights)]
        top = values[0]
        for value in values[1:]:
            top = jnp.maximum(top, value)
        if state:
            old_top, old_sum = state[0][whole, :], state[1][whole, :]
            top = jnp.maximum(top, old_top)
        total = jnp.exp(values[0] - top)
        for value in values[1:]:
            total = total + jnp.exp(value - top)
        if state:
            total = total + old_sum * jnp.exp(old_top - top)
        if len(out) == 1:
            out[0][rows, :] = top + jnp.log(total)
        else:
            out[0][rows, :] = top
            out[1][rows, :] = total
        return carry

    lax.fori_loop(0, score_ref.shape[1] // STRIP, strip, 0, unroll=True)


def unpack(refs, side):
    patches, weights = [], []
    for ref in refs:
        places = [()] if len(ref.shape) == 2 else [(i,) for i in range(ref.shape[0])]
        for place in places:
            patches.append(ref[place + (slice(0, side), slice(None))])
            weights.append(ref[place + (slice(side, side + 1), slice(0, 1))])
    return patches, weights


def all_strips(spec_ref, score_ref):
    return range(score_ref.shape[1] // spec_ref.shape[-1])


def first_kernel(n_in, *refs):
    tab_ref, packs = refs[4], refs[5 : 5 + n_in]
    spec_ref, *out, half_ref, patch_ref, score_ref = refs[5 + n_in :]
    image_spectra(*refs[:5], spec_ref)
    patches, weights = unpack(packs, spec_ref.shape[-1])
    transform(patches, tab_ref, half_ref, patch_ref)
    correlate(spec_ref, tab_ref, patch_ref, all_strips(spec_ref, score_ref), score_ref)
    fold(score_ref, weights, (), 0, out)


def next_kernel(n_in, *refs):
    spec_ref, *state, tab_ref = refs[:4]
    packs, (*out, half_ref, patch_ref, score_ref) = refs[4 : 4 + n_in], refs[4 + n_in :]
    patches, weights = unpack(packs, spec_ref.shape[-1])
    transform(patches, tab_ref, half_ref, patch_ref)
    correlate(spec_ref, tab_ref, patch_ref, all_strips(spec_ref, score_ref), score_ref)
    fold(score_ref, weights, state, 0, out)


def strip_kernel(n_in, strip, *refs):
    spec_ref, *state, tab_ref = refs[:4]
    packs, refs = refs[4 : 4 + n_in], refs[4 + n_in :]
    side = spec_ref.shape[-1]
    patches, weights = unpack(packs, side)
    if strip == 0:
        log_ref, patch_ref, half_ref, score_ref = refs
        transform(patches, tab_ref, half_ref, patch_ref)
    else:
        patch_ref, log_ref, score_ref = refs
    correlate(spec_ref, tab_ref, patch_ref, [strip], score_ref)
    fold(score_ref, weights, state, strip * side, [log_ref])


def folded(stored, side):
    within = stored % side
    return stored - within + jnp.where(within < side // 2, within + side // 2, side - 1 - within)


def keeper(row, side):
    within = row % side
    return row - within + jnp.where(within < side // 2, side - 1 - within, within - side // 2)


def pixel_kernel(side, mask_ref, pixel_ref):
    blocks = (1.0 - mask_ref[...].astype(F32)).astype(BF16)
    rows, cols = blocks.shape
    pixel = folded(lax.broadcasted_iota(jnp.int32, (rows * MBLK, rows), 0), side)
    block = lax.broadcasted_iota(jnp.int32, (rows * MBLK, rows), 1)
    down = (pixel // MBLK == block).astype(F32).astype(BF16)
    pixel = lax.broadcasted_iota(jnp.int32, (cols, cols * MBLK), 1)
    block = lax.broadcasted_iota(jnp.int32, (cols, cols * MBLK), 0)
    across = (pixel // MBLK == block).astype(F32).astype(BF16)
    pixel_ref[...] = product(product(down, blocks).astype(BF16), across)


def join_kernel(n_strip, *refs):
    parts, (pixel_ref, log_ref, stat_ref) = refs[:-3], refs[-3:]
    values = jnp.concatenate([ref[...] for ref in parts[:n_strip]], axis=0)
    if len(parts) > n_strip:
        other = jnp.concatenate([ref[...] for ref in parts[n_strip:]], axis=0)
        top = jnp.maximum(values, other)
        values = top + jnp.log(1.0 + jnp.exp(jnp.minimum(values, other) - top))
    log_ref[...] = values
    pixels = pixel_ref[...]
    count = jnp.sum(pixels)
    total = jnp.sum(pixels * values)
    deviation = values - total / jnp.maximum(count, 1.0)
    squares = jnp.sum(pixels * deviation * deviation)
    lane = lax.broadcasted_iota(jnp.int32, stat_ref.shape, 1)
    stat_ref[...] = jnp.where(lane == 0, count, jnp.where(lane == 1, total, squares))


def own_rows_kernel(side, place_ref, log_ref, pixel_ref, part_ref, open_ref):
    share = part_ref.shape[0]

    def unfold(i, carry):
        row = keeper(place_ref[0] * share + i, side)
        part_ref[pl.ds(i, 1), :] = log_ref[pl.ds(row, 1), :]
        open_ref[pl.ds(i, 1), :] = pixel_ref[pl.ds(row, 1), :]
        return carry

    lax.fori_loop(0, share, unfold, 0, unroll=8)


def norm_kernel(part_ref, open_ref, *refs):
    stats, out_ref = refs[:-1], refs[-1]
    counts = [ref[:, 0:1] for ref in stats]
    totals = [ref[:, 1:2] for ref in stats]
    count, total = sum(counts), sum(totals)
    average = total / count
    squares = 0.0
    for ref, n, s in zip(stats, counts, totals):
        apart = s / jnp.maximum(n, 1.0) - average
        squares = squares + ref[:, 2:3] + n * apart * apart
    scale = 1.0 / jnp.sqrt(squares / count + 1e-05)
    out_ref[...] = open_ref[...] * (part_ref[...] - average[0:1]) * scale[0:1]


def shift(i, step, n):
    return i ^ step if n & (n - 1) == 0 else (i + step) % n


def peer(x, axis, step):
    n = lax.axis_size(axis)
    return lax.ppermute(x, axis, [(i, shift(i, step, n)) for i in range(n)])


def swap(x, axis):
    return lax.ppermute(x, axis, [(i, i ^ 1) for i in range(lax.axis_size(axis))])


def exchange(x, axis, start):
    pairs = [(i, i + 1) for i in range(start, lax.axis_size(axis) - 1, 2)]
    return lax.ppermute(x, axis, pairs + [(j, i) for i, j in pairs])


def pack_kernel(ids_ref, weight_ref, patch_ref, pack_ref, own_id, weights, sems):
    side = patch_ref.shape[0]
    pairs = ((patch_ref, pack_ref.at[0:side]), (weight_ref, weights), (ids_ref, own_id))
    copies = [pltpu.make_async_copy(source, target, sems.at[i]) for i, (source, target) in enumerate(pairs)]
    for copy in copies:
        copy.start()
    for copy in copies:
        copy.wait()
    catalog = lax.broadcasted_iota(jnp.int32, weights.shape, 1)
    weight = jnp.sum(jnp.where(catalog == own_id[...], weights[...], 0.0), axis=1, keepdims=True)
    pack_ref[side:, :] = jnp.broadcast_to(weight, (PACK, side))


def edge_kernel(spot_ref, own_ref, tab_ref, inner_ref, outer_ref):
    half = own_ref.shape[0] // 2
    own = own_ref[...]
    edges = [own[:, :GUARD], own[:, own.shape[1] - GUARD :]]
    left, right = [jnp.concatenate([x[:half], x[half:]], axis=1) for x in edges]
    odd = spot_ref[0] % 2 == 1
    inner_ref[...] = jnp.where(odd, left, right)
    outer_ref[...] = jnp.where(odd, right, left)


def stack_kernel(*refs):
    for i, ref in enumerate(refs[:-1]):
        refs[-1][i] = ref[...]


def cost(micros):
    return pl.CostEstimate(flops=int(micros * 1e9), bytes_accessed=0, transcendentals=0)


def body(micrograph, templates, orient_ids, log_weight, ice_mask):
    side = templates.shape[2]
    tile = micrograph.shape[1]
    blocks = (tile // side) ** 2
    tab = jnp.asarray(tables(side))
    n_tile, n_orient = lax.axis_size("tile"), lax.axis_size("orient")
    place = lax.axis_index("orient").astype(jnp.int32).reshape(1)
    spot = lax.axis_index("tile").astype(jnp.int32).reshape(1)
    pack = pl.pallas_call(
        pack_kernel,
        out_shape=jax.ShapeDtypeStruct((side + PACK, side), F32),
        in_specs=[pl.BlockSpec(memory_space=pl.ANY)] * 3,
        out_specs=VMEM,
        scratch_shapes=[
            pltpu.VMEM((1, 1), jnp.int32),
            pltpu.VMEM((1, log_weight.shape[0]), F32),
            pltpu.SemaphoreType.DMA((3,)),
        ],
        compiler_params=params(60),
        cost_estimate=cost(1),
        name="pack_weight",
    )(orient_ids, log_weight.reshape(1, -1), templates.reshape(side, side))
    micrograph, pack = lax.optimization_barrier((micrograph, pack))
    edge = jax.ShapeDtypeStruct((micrograph.shape[0] // 2, 2 * GUARD), F32)
    inner_edge, outer_edge = pl.pallas_call(
        edge_kernel,
        out_shape=(edge, edge),
        in_specs=[SMEM, VMEM, VMEM],
        out_specs=(VMEM, VMEM),
        compiler_params=params(4),
        cost_estimate=cost(0.5),
        name="edges",
    )(spot, micrograph, tab)

    tile_pairs, orient_pairs = n_tile % 2 == 0, n_orient % 2 == 0
    tile_steps = range(0, n_tile, 2 if tile_pairs else 1)
    orient_steps = range(0, n_orient, 2 if orient_pairs else 1)
    far = [peer(pack, "orient", o) for o in orient_steps[1:]]
    inner, outer = exchange(inner_edge, "tile", 0), exchange(outer_edge, "tile", 1)
    mine = [pack] + ([swap(pack, "tile")] if tile_pairs else [])
    held = pl.pallas_call(
        stack_kernel,
        out_shape=jax.ShapeDtypeStruct((1 + len(far), *pack.shape), F32),
        in_specs=[VMEM] * (1 + len(far)),
        out_specs=VMEM,
        compiler_params=params(4),
        cost_estimate=cost(0.2),
        name="stack_packs",
    )(pack, *far)
    near = [peer(held, "tile", t) for t in tile_steps[1:]]
    early = far + ([swap(x, "tile") for x in far] if tile_pairs else [])

    plane = jax.ShapeDtypeStruct((tile, tile), F32)

    half_shape, patch_shape = (3 * side, 2 * side), (4, side, side)

    def size(arrays):
        return sum(x.shape[0] if x.ndim == 3 else 1 for x in arrays)

    def scratch(n):
        return [pltpu.VMEM((n, *half_shape), BF16), pltpu.VMEM((n, *patch_shape), F32), pltpu.VMEM((n, tile, tile), F32)]

    spec, *state = pl.pallas_call(
        functools.partial(first_kernel, len(mine)),
        out_shape=(jax.ShapeDtypeStruct((blocks, 4, side, side), F32), plane, plane),
        in_specs=[SMEM] + [VMEM] * (4 + len(mine)),
        out_specs=(VMEM,) * 3,
        scratch_shapes=scratch(len(mine)),
        compiler_params=params(24),
        cost_estimate=cost(5 * COST),
        name="own_block",
    )(spot, inner, micrograph, outer, tab, *mine)
    early, state = lax.optimization_barrier((early, state))

    def score(state, arrays):
        count = size(arrays)
        return pl.pallas_call(
            functools.partial(next_kernel, len(arrays)),
            out_shape=(plane,) * 2,
            in_specs=[VMEM] * (4 + len(arrays)),
            out_specs=(VMEM,) * 2,
            scratch_shapes=scratch(count),
            compiler_params=params(24),
            cost_estimate=cost(COST * count),
            name="next_block",
        )(spec, *state, tab, *arrays)

    for i in range(0, len(early), CHUNK):
        state = score(state, early[i : i + CHUNK])
    if near:
        near, state = lax.optimization_barrier((near, state))
    rest = near + ([swap(x, "tile") for x in near] if tile_pairs else [])
    groups = [[]]
    for x in rest or [pack[None]]:
        if groups[-1] and size(groups[-1]) + size([x]) > CHUNK:
            groups.append([])
        groups[-1].append(x)
    for group in groups[:-1]:
        state = score(state, group)
    group = groups[-1]
    count = size(group)
    n_strip = tile // side
    strip_shape = jax.ShapeDtypeStruct((side, tile), F32)
    strip_scratch = pltpu.VMEM((count, side, tile), F32)
    log_map, *spectra = pl.pallas_call(
        functools.partial(strip_kernel, len(group), 0),
        out_shape=(strip_shape, jax.ShapeDtypeStruct((count, *patch_shape), F32)),
        in_specs=[VMEM] * (4 + len(group)),
        out_specs=(VMEM,) * 2,
        scratch_shapes=[pltpu.VMEM((count, *half_shape), BF16), strip_scratch],
        compiler_params=params(24),
        cost_estimate=cost(COST * count),
        name="first_strip",
    )(spec, *state, tab, *group)
    log_maps = [log_map]
    for strip in range(1, n_strip):
        log_maps.append(
            pl.pallas_call(
                functools.partial(strip_kernel, len(group), strip),
                out_shape=strip_shape,
                in_specs=[VMEM] * (5 + len(group)),
                out_specs=VMEM,
                scratch_shapes=[strip_scratch],
                compiler_params=params(24),
                cost_estimate=cost(COST * count),
                name="next_strip",
            )(spec, *state, tab, *group, *spectra)
        )
    maps = log_maps + ([swap(x, "orient") for x in log_maps] if orient_pairs else [])
    pixels = pl.pallas_call(
        functools.partial(pixel_kernel, side),
        out_shape=plane,
        in_specs=[VMEM],
        out_specs=VMEM,
        compiler_params=params(4),
        cost_estimate=cost(1),
        name="open_pixels",
    )(ice_mask)
    log_total, stat = pl.pallas_call(
        functools.partial(join_kernel, n_strip),
        out_shape=(plane, jax.ShapeDtypeStruct((8, LANES), F32)),
        in_specs=[VMEM] * (1 + len(maps)),
        out_specs=(VMEM,) * 2,
        compiler_params=params(8),
        cost_estimate=cost(1),
        name="join_maps",
    )(*maps, pixels)
    share = tile // n_orient
    part = jax.ShapeDtypeStruct((share, tile), F32)
    part, opened = pl.pallas_call(
        functools.partial(own_rows_kernel, side),
        out_shape=(part, part),
        in_specs=[SMEM, VMEM, VMEM],
        out_specs=(VMEM, VMEM),
        compiler_params=params(4),
        cost_estimate=cost(1),
        name="own_rows",
    )(place, log_total, pixels)
    stats = [stat] + [peer(stat, "tile", k) for k in range(1, n_tile)]
    return pl.pallas_call(
        norm_kernel,
        out_shape=jax.ShapeDtypeStruct((share, tile), F32),
        in_specs=[VMEM] * (2 + len(stats)),
        out_specs=VMEM,
        compiler_params=params(4),
        cost_estimate=cost(1),
        name="normalise",
    )(part, opened, *stats)


def solution(mesh):
    return jax.shard_map(
        body,
        mesh=mesh,
        in_specs=(
            P("group", "tile"),
            P("orient", "tile", None, None),
            P("orient", "tile"),
            P(),
            P("group", "tile"),
        ),
        out_specs=P(("group", "orient"), "tile"),
        check_vma=False,
    )
```

```python
import functools
import math

import jax
import jax.numpy as jnp
import ml_dtypes
import numpy as np
from jax import lax
from jax.experimental import pallas as pl
from jax.experimental.pallas import tpu as pltpu
from jax.sharding import PartitionSpec as P

GUARD = 64
MBLK = 16
LANES = 128
PACK = 8
CHUNK = 8
COST = 0.1
OWN, EARLY, REST, LAST = 1, 0.2, 0.4, 2

F32 = jnp.float32
BF16 = jnp.bfloat16
VMEM = pl.BlockSpec(memory_space=pltpu.VMEM)
SMEM = pl.BlockSpec(memory_space=pltpu.SMEM)


def params(mib):
    return pltpu.CompilerParams(vmem_limit_bytes=mib * 2**20)


def high_low(table):
    high = table.astype(np.float32).astype(ml_dtypes.bfloat16)
    low = (table - high.astype(np.float64)).astype(np.float32).astype(ml_dtypes.bfloat16)
    return high, low


def tables(side):
    span = 2 * side
    turn = 2.0 * math.pi * (np.arange(side) + 0.5) / span
    angles = np.outer(np.arange(span), turn)
    high, low = high_low(np.concatenate([np.cos(angles), np.sin(angles)], axis=1))
    middle = np.outer(np.arange(span) - (side - 1) / 2, turn)
    middle_high, middle_low = high_low(np.concatenate([np.cos(middle), np.sin(middle)], axis=1).T)
    away = np.outer(np.arange(side // 2) + 0.5, turn)
    ends = []
    for wave in (np.cos(away), np.sin(away)):
        wave_high, wave_low = high_low(wave)
        ends += [np.concatenate([wave_high, wave_high], axis=1), np.concatenate([wave_low, wave_low], axis=1)]
    return np.concatenate([high, low, high.T, low.T, *ends, middle_high, middle_low], axis=0)


def tall(tab_ref, count):
    span = tab_ref.shape[1]
    high, low = tab_ref[0:count, :], tab_ref[span : span + count, :]
    return jnp.concatenate([high, high, low], axis=0)


def wide(high, low):
    return jnp.concatenate([high, high, low], axis=1)


def back_cols(tab_ref, side):
    span = tab_ref.shape[1]
    both = jnp.concatenate([tab_ref[2 * span : 3 * span, 0:side], tab_ref[3 * span : 4 * span, 0:side]], axis=1)
    return jnp.concatenate([both, both], axis=0)


def split(x):
    high = x.astype(BF16)
    return high, (x - high.astype(F32)).astype(BF16)


def tripled(x, axis):
    high, low = split(x)
    return jnp.concatenate([high, low, high], axis=axis)


def doubled(x, axis):
    return jnp.concatenate(split(x), axis=axis)


def halves(x, axis):
    half = x.shape[axis] // 2
    return x[:half] + x[half:] if axis == 0 else x[:, :half] + x[:, half:]


def product(left, right):
    return jnp.dot(left, right, preferred_element_type=F32)


def paired(quads, side):
    cc, cs = quads[:side, :side], quads[:side, side:]
    sc, ss = quads[side:, :side], quads[side:, side:]
    return cc - ss, sc + cs, cc + ss, sc - cs


def image_spectra(spot_ref, inner_ref, own_ref, outer_ref, tab_ref, spec_ref):
    odd = spot_ref[0] % 2 == 1

    def edge(ref):
        lines = ref[...]
        return jnp.concatenate([lines[:, :GUARD], lines[:, GUARD:]], axis=0)

    inner, outer = edge(inner_ref), edge(outer_ref)
    left, right = jnp.where(odd, inner, outer), jnp.where(odd, outer, inner)
    image = jnp.concatenate([left, own_ref[...], right], axis=1)
    side = spec_ref.shape[-1]
    span = 2 * side
    rows, cols = image.shape[0] // side - 1, image.shape[1] // side - 1
    scale = 2.0 / (span * span)
    cols_table, rows_table = tall(tab_ref, span), wide(tab_ref[5 * span : 6 * span, :], tab_ref[6 * span :, :])
    for q in range(cols):
        half = product(tripled(image[:, q * side : q * side + span], 1), cols_table)
        for p in range(rows):
            full = product(rows_table, tripled(half[p * side : p * side + span], 0))
            for part, value in enumerate(paired(full, side)):
                spec_ref[p * cols + q, part] = value * scale


def transform(patches, tab_ref, half_ref, patch_ref):
    side = patch_ref.shape[-1]
    span = 2 * side
    patch_cols = tall(tab_ref, side)
    patch_rows = wide(tab_ref[2 * span : 3 * span, 0:side], tab_ref[3 * span : 4 * span, 0:side])
    for first in range(0, len(patches), 4):
        group = patches[first : first + 4]
        half = product(tripled(jnp.concatenate(group, axis=0), 1), patch_cols)
        for i in range(len(group)):
            high, low = split(half[i * side : (i + 1) * side])
            half_ref[first + i, 0:side] = high
            half_ref[first + i, side : 2 * side] = low
            half_ref[first + i, 2 * side : 3 * side] = high

    def finish(n, carry):
        for part, value in enumerate(paired(product(patch_rows, half_ref[n]), side)):
            patch_ref[n, part] = value
        return carry

    lax.fori_loop(0, len(patches), finish, 0, unroll=steps_at_once(len(patches), 8))


def steps_at_once(count, most):
    return max(u for u in range(1, most + 1) if count % u == 0)


def correlate(spec_ref, tab_ref, patch_refs, strip, score_ref):
    side = spec_ref.shape[-1]
    span = 2 * side
    cols = score_ref.shape[2] // side
    even_rows, odd_rows = tab_ref[4 * span : 4 * span + side, :], tab_ref[4 * span + side : 5 * span, :]
    cols_table = back_cols(tab_ref, side)
    first = 0
    for patch_ref in patch_refs:

        def score(n, carry, patch_ref=patch_ref, first=first):
            tr, tu, sr, si = (patch_ref[n, part] for part in range(4))
            for q in range(cols):
                ir, iu, jr, ji = (spec_ref[strip * cols + q, part] for part in range(4))
                a, b = ir * tr + iu * tu, iu * tr - ir * tu
                c, e = jr * sr + ji * si, jr * si - ji * sr
                top = jnp.concatenate([a + c, e + b], axis=1)
                low = jnp.concatenate([b - e, c - a], axis=1)
                even = halves(product(even_rows, doubled(top, 0)), 0)
                odd = halves(product(odd_rows, doubled(low, 0)), 0)
                lines = jnp.concatenate([even + odd, even - odd], axis=0)
                score_ref[first + n, :, q * side : (q + 1) * side] = halves(product(doubled(lines, 1), cols_table), 1)
            return carry

        count = patch_ref.shape[0]
        lax.fori_loop(0, count, score, 0, unroll=steps_at_once(count, 16 // cols))
        first += count


STRIP = 64


def fold(score_ref, weights, state, out):
    def strip(r, carry):
        rows = pl.ds(pl.multiple_of(r * STRIP, STRIP), STRIP)
        values = [score_ref[n, rows, :] + weight for n, weight in enumerate(weights)]
        top = values[0]
        for value in values[1:]:
            top = jnp.maximum(top, value)
        if state:
            old_top, old_sum = state[0][rows, :], state[1][rows, :]
            top = jnp.maximum(top, old_top)
        total = jnp.exp(values[0] - top)
        for value in values[1:]:
            total = total + jnp.exp(value - top)
        if state:
            total = total + old_sum * jnp.exp(old_top - top)
        if len(out) == 1:
            out[0][rows, :] = top + jnp.log(total)
        else:
            out[0][rows, :] = top
            out[1][rows, :] = total
        return carry

    lax.fori_loop(0, score_ref.shape[1] // STRIP, strip, 0, unroll=True)


def unpack(refs, side):
    patches, weights = [], []
    for ref in refs:
        places = [()] if len(ref.shape) == 2 else [(i,) for i in range(ref.shape[0])]
        for place in places:
            patches.append(ref[place + (slice(0, side), slice(None))])
            weights.append(ref[place + (slice(side, side + 1), slice(0, 1))])
    return patches, weights


def own_kernel(n_in, strip, *refs):
    tab_ref, packs = refs[4], refs[5 : 5 + n_in]
    spec_ref, *out, patch_ref, half_ref, score_ref = refs[5 + n_in :]
    image_spectra(*refs[:5], spec_ref)
    patches, weights = unpack(packs, spec_ref.shape[-1])
    transform(patches, tab_ref, half_ref, patch_ref)
    correlate(spec_ref, tab_ref, [patch_ref], strip, score_ref)
    fold(score_ref, weights, (), out)


def strip_kernel(n_in, n_spectra, n_state, strip, *refs):
    spec_ref, tab_ref, refs = refs[0], refs[1], refs[2:]
    state, packs, refs = refs[:n_state], refs[n_state : n_state + n_in], refs[n_state + n_in :]
    patches, weights = unpack(packs, spec_ref.shape[-1])
    if n_spectra:
        patch_refs, (*out, score_ref) = refs[:n_spectra], refs[n_spectra:]
    else:
        *out, patch_ref, half_ref, score_ref = refs
        transform(patches, tab_ref, half_ref, patch_ref)
        patch_refs = [patch_ref]
    correlate(spec_ref, tab_ref, patch_refs, strip, score_ref)
    fold(score_ref, weights, state, out)


def folded(stored, side):
    within = stored % side
    return stored - within + jnp.where(within < side // 2, within + side // 2, side - 1 - within)


def keeper(row, side):
    within = row % side
    return row - within + jnp.where(within < side // 2, side - 1 - within, within - side // 2)


def pixel_kernel(side, mask_ref, pixel_ref):
    blocks = (1.0 - mask_ref[...].astype(F32)).astype(BF16)
    rows, cols = blocks.shape
    pixel = folded(lax.broadcasted_iota(jnp.int32, (rows * MBLK, rows), 0), side)
    block = lax.broadcasted_iota(jnp.int32, (rows * MBLK, rows), 1)
    down = (pixel // MBLK == block).astype(F32).astype(BF16)
    pixel = lax.broadcasted_iota(jnp.int32, (cols, cols * MBLK), 1)
    block = lax.broadcasted_iota(jnp.int32, (cols, cols * MBLK), 0)
    across = (pixel // MBLK == block).astype(F32).astype(BF16)
    pixel_ref[...] = product(product(down, blocks).astype(BF16), across)


def join_kernel(n_map, strip, *refs):
    maps, (pixel_ref, *before, log_ref, stat_ref) = refs[:n_map], refs[n_map:]
    values = maps[0][...]
    for ref in maps[1:]:
        other = ref[...]
        top = jnp.maximum(values, other)
        values = top + jnp.log(1.0 + jnp.exp(jnp.minimum(values, other) - top))
    log_ref[...] = values
    side = values.shape[0]
    pixels = pixel_ref[strip * side : (strip + 1) * side, :]
    count = jnp.sum(pixels)
    total = jnp.sum(pixels * values)
    deviation = values - total / jnp.maximum(count, 1.0)
    squares = jnp.sum(pixels * deviation * deviation)
    lane = lax.broadcasted_iota(jnp.int32, stat_ref.shape, 1)
    stat = before[0][...] if before else jnp.zeros(stat_ref.shape, F32)
    for i, value in enumerate((count, total, squares)):
        stat = jnp.where(lane == 3 * strip + i, value, stat)
    stat_ref[...] = stat


def own_rows_kernel(n_strip, place_ref, *refs):
    strips, (pixel_ref, part_ref, open_ref, log_ref) = refs[:n_strip], refs[n_strip:]
    side = strips[0].shape[0]
    share = part_ref.shape[0]
    for i, ref in enumerate(strips):
        log_ref[i * side : (i + 1) * side, :] = ref[...]

    def unfold(i, carry):
        row = keeper(place_ref[0] * share + i, side)
        part_ref[pl.ds(i, 1), :] = log_ref[pl.ds(row, 1), :]
        open_ref[pl.ds(i, 1), :] = pixel_ref[pl.ds(row, 1), :]
        return carry

    lax.fori_loop(0, share, unfold, 0, unroll=8)


def norm_kernel(n_strip, part_ref, open_ref, *refs):
    stats, out_ref = refs[:-1], refs[-1]
    lanes = [(ref, 3 * strip) for ref in stats for strip in range(n_strip)]
    counts = [ref[:, i : i + 1] for ref, i in lanes]
    totals = [ref[:, i + 1 : i + 2] for ref, i in lanes]
    count, total = sum(counts), sum(totals)
    average = total / count
    squares = 0.0
    for (ref, i), n, s in zip(lanes, counts, totals):
        apart = s / jnp.maximum(n, 1.0) - average
        squares = squares + ref[:, i + 2 : i + 3] + n * apart * apart
    scale = 1.0 / jnp.sqrt(squares / count + 1e-05)
    out_ref[...] = open_ref[...] * (part_ref[...] - average[0:1]) * scale[0:1]


def shift(i, step, n):
    return i ^ step if n & (n - 1) == 0 else (i + step) % n


def peer(x, axis, step):
    n = lax.axis_size(axis)
    return lax.ppermute(x, axis, [(i, shift(i, step, n)) for i in range(n)])


def swap(x, axis):
    return lax.ppermute(x, axis, [(i, i ^ 1) for i in range(lax.axis_size(axis))])


def exchange(x, axis, start):
    pairs = [(i, i + 1) for i in range(start, lax.axis_size(axis) - 1, 2)]
    return lax.ppermute(x, axis, pairs + [(j, i) for i, j in pairs])


def pack_kernel(ids_ref, weight_ref, patch_ref, pack_ref, weights, sems):
    side = patch_ref.shape[0]
    pairs = ((patch_ref, pack_ref.at[0:side]), (weight_ref, weights))
    copies = [pltpu.make_async_copy(source, target, sems.at[i]) for i, (source, target) in enumerate(pairs)]
    for copy in copies:
        copy.start()
    for copy in copies:
        copy.wait()
    catalog = lax.broadcasted_iota(jnp.int32, weights.shape, 1)
    weight = jnp.sum(jnp.where(catalog == ids_ref[0, 0], weights[...], 0.0), axis=1, keepdims=True)
    pack_ref[side:, :] = jnp.broadcast_to(weight, (PACK, side))


def edge_kernel(spot_ref, own_ref, tab_ref, inner_ref, outer_ref):
    half = own_ref.shape[0] // 2
    own = own_ref[...]
    edges = [own[:, :GUARD], own[:, own.shape[1] - GUARD :]]
    left, right = [jnp.concatenate([x[:half], x[half:]], axis=1) for x in edges]
    odd = spot_ref[0] % 2 == 1
    inner_ref[...] = jnp.where(odd, left, right)
    outer_ref[...] = jnp.where(odd, right, left)


def stack_kernel(*refs):
    for i, ref in enumerate(refs[:-1]):
        refs[-1][i] = ref[...]


def cost(micros):
    return pl.CostEstimate(flops=int(micros * 1e9), bytes_accessed=0, transcendentals=0)


def body(micrograph, templates, orient_ids, log_weight, ice_mask):
    side = templates.shape[2]
    tile = micrograph.shape[1]
    blocks = (tile // side) ** 2
    tab = jnp.asarray(tables(side))
    n_tile, n_orient = lax.axis_size("tile"), lax.axis_size("orient")
    place = lax.axis_index("orient").astype(jnp.int32).reshape(1)
    spot = lax.axis_index("tile").astype(jnp.int32).reshape(1)
    stay = [pltpu.with_memory_space_constraint(x, pltpu.HBM) for x in (log_weight.reshape(1, -1), templates.reshape(side, side))]
    pack = pl.pallas_call(
        pack_kernel,
        out_shape=jax.ShapeDtypeStruct((side + PACK, side), F32),
        in_specs=[SMEM, pl.BlockSpec(memory_space=pltpu.HBM), pl.BlockSpec(memory_space=pltpu.HBM)],
        out_specs=VMEM,
        scratch_shapes=[pltpu.VMEM((1, log_weight.shape[0]), F32), pltpu.SemaphoreType.DMA((2,))],
        compiler_params=params(4),
        cost_estimate=cost(1),
        name="pack_weight",
    )(orient_ids, *stay)
    micrograph, pack = lax.optimization_barrier((micrograph, pack))
    edge = jax.ShapeDtypeStruct((micrograph.shape[0] // 2, 2 * GUARD), F32)
    inner_edge, outer_edge = pl.pallas_call(
        edge_kernel,
        out_shape=(edge, edge),
        in_specs=[SMEM, VMEM, VMEM],
        out_specs=(VMEM, VMEM),
        compiler_params=params(4),
        cost_estimate=cost(0.5),
        name="edges",
    )(spot, micrograph, tab)

    tile_pairs, orient_pairs = n_tile % 2 == 0, n_orient % 2 == 0
    tile_steps = range(0, n_tile, 2 if tile_pairs else 1)
    orient_steps = range(0, n_orient, 2 if orient_pairs else 1)
    far = [peer(pack, "orient", o) for o in orient_steps[1:]]
    inner, outer = exchange(inner_edge, "tile", 0), exchange(outer_edge, "tile", 1)
    mine = [pack] + ([swap(pack, "tile")] if tile_pairs else [])

    plane = jax.ShapeDtypeStruct((tile, tile), F32)

    strip_shape = jax.ShapeDtypeStruct((side, tile), F32)
    half_shape, patch_shape = (3 * side, 2 * side), (4, side, side)

    def size(arrays):
        return sum(x.shape[0] if x.ndim == 3 else 1 for x in arrays)

    def call(kernel, name, micros, shapes, scratch, *operands, places=(), mib=24):
        return pl.pallas_call(
            kernel,
            out_shape=shapes,
            in_specs=[SMEM] * len(places) + [VMEM] * len(operands),
            out_specs=jax.tree.map(lambda _: VMEM, shapes),
            scratch_shapes=scratch,
            compiler_params=params(mib),
            cost_estimate=cost(micros),
            name=name,
        )(*places, *operands)

    def spectra_shape(count):
        return jax.ShapeDtypeStruct((count, *patch_shape), F32)

    def halves_scratch(count):
        return pltpu.VMEM((count, *half_shape), BF16)

    def score_scratch(count):
        return pltpu.VMEM((count, side, tile), F32)

    n_strip = tile // side
    held = call(stack_kernel, "stack_packs", COST, jax.ShapeDtypeStruct((1 + len(far), *pack.shape), F32), [], pack, *far)
    near = [peer(held, "tile", t) for t in tile_steps[1:]]
    early = far + ([swap(x, "tile") for x in far] if tile_pairs else [])
    spec, *state, own_spectra = call(
        functools.partial(own_kernel, len(mine), 0),
        "own_block",
        OWN,
        (jax.ShapeDtypeStruct((blocks, 4, side, side), F32), strip_shape, strip_shape, spectra_shape(len(mine))),
        [halves_scratch(len(mine)), score_scratch(len(mine))],
        inner,
        micrograph,
        outer,
        tab,
        *mine,
        places=(spot,),
    )

    def score(arrays, spectra, state, strip, last, micros):
        count = size(arrays)
        shapes = (strip_shape,) * (1 if last else 2)
        scratch = [score_scratch(count)]
        if not spectra:
            shapes += (spectra_shape(count),)
            scratch = [halves_scratch(count)] + scratch
        out = call(
            functools.partial(strip_kernel, len(arrays), len(spectra), len(state), strip),
            "score_strip",
            micros,
            shapes,
            scratch,
            spec,
            tab,
            *state,
            *arrays,
            *spectra,
        )
        return (out, spectra) if spectra else (out[:-1], [out[-1]])

    def chunks(arrays):
        groups = []
        for x in arrays:
            if not groups or size(groups[-1]) + size([x]) > CHUNK:
                groups.append([])
            groups[-1].append(x)
        return groups

    done = [(mine, [own_spectra])]
    early, state = lax.optimization_barrier((early, state))
    for group in chunks(early):
        state, spectra = score(group, [], state, 0, False, EARLY)
        done.append((group, spectra))
    near, state = lax.optimization_barrier((near, state))
    groups = chunks(near + ([swap(x, "tile") for x in near] if tile_pairs else []))
    for i, group in enumerate(groups):
        state, spectra = score(group, [], state, 0, i == len(groups) - 1, REST)
        done.append((group, spectra))
    log_maps = [state[0]]
    swapped = [swap(state[0], "orient")] if orient_pairs else []
    if sum(size(arrays) for arrays, _ in done) <= CHUNK:
        done = [([x for arrays, _ in done for x in arrays], [x for _, spectra in done for x in spectra])]
    for strip in range(1, n_strip):
        state = ()
        for i, (arrays, spectra) in enumerate(done):
            state, _ = score(arrays, spectra, state, strip, i == len(done) - 1, LAST)
        log_maps.append(state[0])
        if orient_pairs:
            swapped.append(swap(state[0], "orient"))
    pixels = call(functools.partial(pixel_kernel, side), "open_pixels", 1, plane, [], ice_mask)
    stat_shape = jax.ShapeDtypeStruct((8, LANES), F32)
    stat, strips = (), []
    for strip, maps in enumerate(zip(log_maps, swapped) if orient_pairs else zip(log_maps)):
        joined, *stat = call(
            functools.partial(join_kernel, len(maps), strip),
            "join_maps",
            COST,
            (strip_shape, stat_shape),
            [],
            *maps,
            pixels,
            *stat,
        )
        strips.append(joined)
    stat = stat[0]
    share = tile // n_orient
    part = jax.ShapeDtypeStruct((share, tile), F32)
    part, opened = call(
        functools.partial(own_rows_kernel, n_strip),
        "own_rows",
        1,
        (part, part),
        [pltpu.VMEM((tile, tile), F32)],
        *strips,
        pixels,
        places=(place,),
    )
    stats = [stat] + [peer(stat, "tile", k) for k in range(1, n_tile)]
    return call(
        functools.partial(norm_kernel, n_strip),
        "normalise",
        1,
        jax.ShapeDtypeStruct((share, tile), F32),
        [],
        part,
        opened,
        *stats,
    )


def solution(mesh):
    return jax.shard_map(
        body,
        mesh=mesh,
        in_specs=(
            P("group", "tile"),
            P("orient", "tile", None, None),
            P("orient", "tile"),
            P(),
            P("group", "tile"),
        ),
        out_specs=P(("group", "orient"), "tile"),
        check_vma=False,
    )
```

```python
import functools
import math

import jax
import jax.numpy as jnp
import ml_dtypes
import numpy as np
from jax import lax
from jax.experimental import pallas as pl
from jax.experimental.pallas import tpu as pltpu
from jax.sharding import PartitionSpec as P

GUARD = 64
MBLK = 16
LANES = 128
PACK = 8
CHUNK = 8
COST = 0.1
OWN, EARLY, REST, LAST = 1, 0.2, 0.4, 2

F32 = jnp.float32
BF16 = jnp.bfloat16
VMEM = pl.BlockSpec(memory_space=pltpu.VMEM)
SMEM = pl.BlockSpec(memory_space=pltpu.SMEM)


def params(mib):
    return pltpu.CompilerParams(vmem_limit_bytes=mib * 2**20)


def high_low(table):
    high = table.astype(np.float32).astype(ml_dtypes.bfloat16)
    low = (table - high.astype(np.float64)).astype(np.float32).astype(ml_dtypes.bfloat16)
    return high, low


def tables(side):
    span = 2 * side
    turn = 2.0 * math.pi * (np.arange(side) + 0.5) / span
    angles = np.outer(np.arange(span), turn)
    high, low = high_low(np.concatenate([np.cos(angles), np.sin(angles)], axis=1))
    middle = np.outer(np.arange(span) - (side - 1) / 2, turn)
    middle_high, middle_low = high_low(np.concatenate([np.cos(middle), np.sin(middle)], axis=1).T)
    away = np.outer(np.arange(side // 2) + 0.5, turn)
    ends = []
    for wave in (np.cos(away), np.sin(away)):
        wave_high, wave_low = high_low(wave)
        ends += [np.concatenate([wave_high, wave_high], axis=1), np.concatenate([wave_low, wave_low], axis=1)]
    return np.concatenate([high, low, high.T, low.T, *ends, middle_high, middle_low], axis=0)


def tall(tab_ref, count):
    span = tab_ref.shape[1]
    high, low = tab_ref[0:count, :], tab_ref[span : span + count, :]
    return jnp.concatenate([high, high, low], axis=0)


def wide(high, low):
    return jnp.concatenate([high, high, low], axis=1)


def back_cols(tab_ref, side):
    span = tab_ref.shape[1]
    both = jnp.concatenate([tab_ref[2 * span : 3 * span, 0:side], tab_ref[3 * span : 4 * span, 0:side]], axis=1)
    return jnp.concatenate([both, both], axis=0)


def split(x):
    high = x.astype(BF16)
    return high, (x - high.astype(F32)).astype(BF16)


def tripled(x, axis):
    high, low = split(x)
    return jnp.concatenate([high, low, high], axis=axis)


def doubled(x, axis):
    return jnp.concatenate(split(x), axis=axis)


def halves(x, axis):
    half = x.shape[axis] // 2
    return x[:half] + x[half:] if axis == 0 else x[:, :half] + x[:, half:]


def product(left, right):
    return jnp.dot(left, right, preferred_element_type=F32)


def paired(quads, side):
    cc, cs = quads[:side, :side], quads[:side, side:]
    sc, ss = quads[side:, :side], quads[side:, side:]
    return cc - ss, sc + cs, cc + ss, sc - cs


def image_spectra(spot_ref, inner_ref, own_ref, outer_ref, tab_ref, spec_ref):
    odd = spot_ref[0] % 2 == 1

    def edge(ref):
        lines = ref[...]
        return jnp.concatenate([lines[:, :GUARD], lines[:, GUARD:]], axis=0)

    inner, outer = edge(inner_ref), edge(outer_ref)
    left, right = jnp.where(odd, inner, outer), jnp.where(odd, outer, inner)
    image = jnp.concatenate([left, own_ref[...], right], axis=1)
    side = spec_ref.shape[-1]
    span = 2 * side
    rows, cols = image.shape[0] // side - 1, image.shape[1] // side - 1
    scale = 2.0 / (span * span)
    cols_table, rows_table = tall(tab_ref, span), wide(tab_ref[5 * span : 6 * span, :], tab_ref[6 * span :, :])
    for q in range(cols):
        half = product(tripled(image[:, q * side : q * side + span], 1), cols_table)
        for p in range(rows):
            full = product(rows_table, tripled(half[p * side : p * side + span], 0))
            for part, value in enumerate(paired(full, side)):
                spec_ref[p * cols + q, part] = value * scale


def transform(patches, tab_ref, half_ref, patch_ref):
    side = patch_ref.shape[-1]
    span = 2 * side
    patch_cols = tall(tab_ref, side)
    patch_rows = wide(tab_ref[2 * span : 3 * span, 0:side], tab_ref[3 * span : 4 * span, 0:side])
    for first in range(0, len(patches), 4):
        group = patches[first : first + 4]
        half = product(tripled(jnp.concatenate(group, axis=0), 1), patch_cols)
        for i in range(len(group)):
            high, low = split(half[i * side : (i + 1) * side])
            half_ref[first + i, 0:side] = high
            half_ref[first + i, side : 2 * side] = low
            half_ref[first + i, 2 * side : 3 * side] = high

    def finish(n, carry):
        for part, value in enumerate(paired(product(patch_rows, half_ref[n]), side)):
            patch_ref[n, part] = value
        return carry

    lax.fori_loop(0, len(patches), finish, 0, unroll=steps_at_once(len(patches), 8))


def steps_at_once(count, most):
    return max(u for u in range(1, most + 1) if count % u == 0)


def correlate(spec_ref, tab_ref, patch_refs, strip, score_ref):
    side = spec_ref.shape[-1]
    span = 2 * side
    cols = score_ref.shape[2] // side
    even_rows, odd_rows = tab_ref[4 * span : 4 * span + side, :], tab_ref[4 * span + side : 5 * span, :]
    cols_table = back_cols(tab_ref, side)
    first = 0
    for patch_ref in patch_refs:

        def score(n, carry, patch_ref=patch_ref, first=first):
            tr, tu, sr, si = (patch_ref[n, part] for part in range(4))
            for q in range(cols):
                ir, iu, jr, ji = (spec_ref[strip * cols + q, part] for part in range(4))
                a, b = ir * tr + iu * tu, iu * tr - ir * tu
                c, e = jr * sr + ji * si, jr * si - ji * sr
                top = jnp.concatenate([a + c, e + b], axis=1)
                low = jnp.concatenate([b - e, c - a], axis=1)
                even = halves(product(even_rows, doubled(top, 0)), 0)
                odd = halves(product(odd_rows, doubled(low, 0)), 0)
                lines = jnp.concatenate([even + odd, even - odd], axis=0)
                score_ref[first + n, :, q * side : (q + 1) * side] = halves(product(doubled(lines, 1), cols_table), 1)
            return carry

        count = patch_ref.shape[0]
        lax.fori_loop(0, count, score, 0, unroll=steps_at_once(count, 16 // cols))
        first += count


STRIP = 64


def fold(score_ref, weights, state, out):
    def strip(r, carry):
        rows = pl.ds(pl.multiple_of(r * STRIP, STRIP), STRIP)
        values = [score_ref[n, rows, :] + weight for n, weight in enumerate(weights)]
        top = values[0]
        for value in values[1:]:
            top = jnp.maximum(top, value)
        if state:
            old_top, old_sum = state[0][rows, :], state[1][rows, :]
            top = jnp.maximum(top, old_top)
        total = jnp.exp(values[0] - top)
        for value in values[1:]:
            total = total + jnp.exp(value - top)
        if state:
            total = total + old_sum * jnp.exp(old_top - top)
        if len(out) == 1:
            out[0][rows, :] = top + jnp.log(total)
        else:
            out[0][rows, :] = top
            out[1][rows, :] = total
        return carry

    lax.fori_loop(0, score_ref.shape[1] // STRIP, strip, 0, unroll=True)


def unpack(refs, side):
    patches, weights = [], []
    for ref in refs:
        places = [()] if len(ref.shape) == 2 else [(i,) for i in range(ref.shape[0])]
        for place in places:
            patches.append(ref[place + (slice(0, side), slice(None))])
            weights.append(ref[place + (slice(side, side + 1), slice(0, 1))])
    return patches, weights


def own_kernel(n_in, strip, *refs):
    tab_ref, packs = refs[4], refs[5 : 5 + n_in]
    spec_ref, *out, patch_ref, half_ref, score_ref = refs[5 + n_in :]
    image_spectra(*refs[:5], spec_ref)
    patches, weights = unpack(packs, spec_ref.shape[-1])
    transform(patches, tab_ref, half_ref, patch_ref)
    correlate(spec_ref, tab_ref, [patch_ref], strip, score_ref)
    fold(score_ref, weights, (), out)


def strip_kernel(n_in, n_spectra, n_state, strip, *refs):
    spec_ref, tab_ref, refs = refs[0], refs[1], refs[2:]
    state, packs, refs = refs[:n_state], refs[n_state : n_state + n_in], refs[n_state + n_in :]
    patches, weights = unpack(packs, spec_ref.shape[-1])
    if n_spectra:
        patch_refs, (*out, score_ref) = refs[:n_spectra], refs[n_spectra:]
    else:
        *out, patch_ref, half_ref, score_ref = refs
        transform(patches, tab_ref, half_ref, patch_ref)
        patch_refs = [patch_ref]
    correlate(spec_ref, tab_ref, patch_refs, strip, score_ref)
    fold(score_ref, weights, state, out)


def folded(stored, side):
    within = stored % side
    return stored - within + jnp.where(within < side // 2, within + side // 2, side - 1 - within)


def keeper(row, side):
    within = row % side
    return row - within + jnp.where(within < side // 2, side - 1 - within, within - side // 2)


def pixel_kernel(side, mask_ref, pixel_ref):
    blocks = (1.0 - mask_ref[...].astype(F32)).astype(BF16)
    rows, cols = blocks.shape
    pixel = folded(lax.broadcasted_iota(jnp.int32, (rows * MBLK, rows), 0), side)
    block = lax.broadcasted_iota(jnp.int32, (rows * MBLK, rows), 1)
    down = (pixel // MBLK == block).astype(F32).astype(BF16)
    pixel = lax.broadcasted_iota(jnp.int32, (cols, cols * MBLK), 1)
    block = lax.broadcasted_iota(jnp.int32, (cols, cols * MBLK), 0)
    across = (pixel // MBLK == block).astype(F32).astype(BF16)
    pixel_ref[...] = product(product(down, blocks).astype(BF16), across)


def join_kernel(n_map, strip, *refs):
    maps, (pixel_ref, *before, log_ref, stat_ref) = refs[:n_map], refs[n_map:]
    values = maps[0][...]
    for ref in maps[1:]:
        other = ref[...]
        top = jnp.maximum(values, other)
        values = top + jnp.log(1.0 + jnp.exp(jnp.minimum(values, other) - top))
    log_ref[...] = values
    side = values.shape[0]
    pixels = pixel_ref[strip * side : (strip + 1) * side, :]
    count = jnp.sum(pixels)
    total = jnp.sum(pixels * values)
    deviation = values - total / jnp.maximum(count, 1.0)
    squares = jnp.sum(pixels * deviation * deviation)
    row = lax.broadcasted_iota(jnp.int32, stat_ref.shape, 0)
    stat = before[0][...] if before else jnp.zeros(stat_ref.shape, F32)
    for i, value in enumerate((count, total, squares)):
        stat = jnp.where(row == 3 * strip + i, value, stat)
    stat_ref[...] = stat


def own_rows_kernel(n_strip, place_ref, *refs):
    strips, (pixel_ref, part_ref, open_ref, log_ref) = refs[:n_strip], refs[n_strip:]
    side = strips[0].shape[0]
    share = part_ref.shape[0]
    for i, ref in enumerate(strips):
        log_ref[i * side : (i + 1) * side, :] = ref[...]

    def unfold(i, carry):
        row = keeper(place_ref[0] * share + i, side)
        part_ref[pl.ds(i, 1), :] = log_ref[pl.ds(row, 1), :]
        open_ref[pl.ds(i, 1), :] = pixel_ref[pl.ds(row, 1), :]
        return carry

    lax.fori_loop(0, share, unfold, 0, unroll=8)


def norm_kernel(n_strip, part_ref, open_ref, *refs):
    stats, out_ref = refs[:-1], refs[-1]
    rows = [(ref[...], 3 * strip) for ref in stats for strip in range(n_strip)]
    counts = [stat[i : i + 1] for stat, i in rows]
    totals = [stat[i + 1 : i + 2] for stat, i in rows]
    count, total = sum(counts), sum(totals)
    average = total / count
    squares = 0.0
    for (stat, i), n, s in zip(rows, counts, totals):
        apart = s / jnp.maximum(n, 1.0) - average
        squares = squares + stat[i + 2 : i + 3] + n * apart * apart
    scale = 1.0 / jnp.sqrt(squares / count + 1e-05)
    for i in range(0, out_ref.shape[1], LANES):
        cols = slice(i, i + LANES)
        out_ref[:, cols] = open_ref[:, cols] * (part_ref[:, cols] - average) * scale


def shift(i, step, n):
    return i ^ step if n & (n - 1) == 0 else (i + step) % n


def peer(x, axis, step):
    n = lax.axis_size(axis)
    return lax.ppermute(x, axis, [(i, shift(i, step, n)) for i in range(n)])


def swap(x, axis):
    return lax.ppermute(x, axis, [(i, i ^ 1) for i in range(lax.axis_size(axis))])


def exchange(x, axis, start):
    pairs = [(i, i + 1) for i in range(start, lax.axis_size(axis) - 1, 2)]
    return lax.ppermute(x, axis, pairs + [(j, i) for i, j in pairs])


def pack_kernel(ids_ref, weight_ref, patch_ref, pack_ref, weights, sems):
    side = patch_ref.shape[0]
    pairs = ((patch_ref, pack_ref.at[0:side]), (weight_ref, weights))
    copies = [pltpu.make_async_copy(source, target, sems.at[i]) for i, (source, target) in enumerate(pairs)]
    for copy in copies:
        copy.start()
    for copy in copies:
        copy.wait()
    catalog = lax.broadcasted_iota(jnp.int32, weights.shape, 1)
    weight = jnp.sum(jnp.where(catalog == ids_ref[0, 0], weights[...], 0.0), axis=1, keepdims=True)
    pack_ref[side:, :] = jnp.broadcast_to(weight, (PACK, side))


def edge_kernel(spot_ref, own_ref, tab_ref, inner_ref, outer_ref):
    half = own_ref.shape[0] // 2
    own = own_ref[...]
    edges = [own[:, :GUARD], own[:, own.shape[1] - GUARD :]]
    left, right = [jnp.concatenate([x[:half], x[half:]], axis=1) for x in edges]
    odd = spot_ref[0] % 2 == 1
    inner_ref[...] = jnp.where(odd, left, right)
    outer_ref[...] = jnp.where(odd, right, left)


def stack_kernel(*refs):
    for i, ref in enumerate(refs[:-1]):
        refs[-1][i] = ref[...]


def cost(micros):
    return pl.CostEstimate(flops=int(micros * 1e9), bytes_accessed=0, transcendentals=0)


def body(micrograph, templates, orient_ids, log_weight, ice_mask):
    side = templates.shape[2]
    tile = micrograph.shape[1]
    blocks = (tile // side) ** 2
    tab = jnp.asarray(tables(side))
    n_tile, n_orient = lax.axis_size("tile"), lax.axis_size("orient")
    place = lax.axis_index("orient").astype(jnp.int32).reshape(1)
    spot = lax.axis_index("tile").astype(jnp.int32).reshape(1)
    stay = [pltpu.with_memory_space_constraint(x, pltpu.HBM) for x in (log_weight.reshape(1, -1), templates.reshape(side, side))]
    pack = pl.pallas_call(
        pack_kernel,
        out_shape=jax.ShapeDtypeStruct((side + PACK, side), F32),
        in_specs=[SMEM, pl.BlockSpec(memory_space=pltpu.HBM), pl.BlockSpec(memory_space=pltpu.HBM)],
        out_specs=VMEM,
        scratch_shapes=[pltpu.VMEM((1, log_weight.shape[0]), F32), pltpu.SemaphoreType.DMA((2,))],
        compiler_params=params(4),
        cost_estimate=cost(1),
        name="pack_weight",
    )(orient_ids, *stay)
    micrograph, pack = lax.optimization_barrier((micrograph, pack))
    edge = jax.ShapeDtypeStruct((micrograph.shape[0] // 2, 2 * GUARD), F32)
    inner_edge, outer_edge = pl.pallas_call(
        edge_kernel,
        out_shape=(edge, edge),
        in_specs=[SMEM, VMEM, VMEM],
        out_specs=(VMEM, VMEM),
        compiler_params=params(4),
        cost_estimate=cost(0.5),
        name="edges",
    )(spot, micrograph, tab)

    tile_pairs, orient_pairs = n_tile % 2 == 0, n_orient % 2 == 0
    tile_steps = range(0, n_tile, 2 if tile_pairs else 1)
    orient_steps = range(0, n_orient, 2 if orient_pairs else 1)
    far = [peer(pack, "orient", o) for o in orient_steps[1:]]
    inner, outer = exchange(inner_edge, "tile", 0), exchange(outer_edge, "tile", 1)
    mine = [pack] + ([swap(pack, "tile")] if tile_pairs else [])

    plane = jax.ShapeDtypeStruct((tile, tile), F32)

    strip_shape = jax.ShapeDtypeStruct((side, tile), F32)
    half_shape, patch_shape = (3 * side, 2 * side), (4, side, side)

    def size(arrays):
        return sum(x.shape[0] if x.ndim == 3 else 1 for x in arrays)

    def call(kernel, name, micros, shapes, scratch, *operands, places=(), mib=24):
        return pl.pallas_call(
            kernel,
            out_shape=shapes,
            in_specs=[SMEM] * len(places) + [VMEM] * len(operands),
            out_specs=jax.tree.map(lambda _: VMEM, shapes),
            scratch_shapes=scratch,
            compiler_params=params(mib),
            cost_estimate=cost(micros),
            name=name,
        )(*places, *operands)

    def spectra_shape(count):
        return jax.ShapeDtypeStruct((count, *patch_shape), F32)

    def halves_scratch(count):
        return pltpu.VMEM((count, *half_shape), BF16)

    def score_scratch(count):
        return pltpu.VMEM((count, side, tile), F32)

    n_strip = tile // side
    held = call(stack_kernel, "stack_packs", COST, jax.ShapeDtypeStruct((1 + len(far), *pack.shape), F32), [], pack, *far)
    relayed = [peer(held, "tile", t) for t in tile_steps[1:]]
    early = far + ([swap(x, "tile") for x in far] if tile_pairs else [])
    spec, *state, own_spectra = call(
        functools.partial(own_kernel, len(mine), 0),
        "own_block",
        OWN,
        (jax.ShapeDtypeStruct((blocks, 4, side, side), F32), strip_shape, strip_shape, spectra_shape(len(mine))),
        [halves_scratch(len(mine)), score_scratch(len(mine))],
        inner,
        micrograph,
        outer,
        tab,
        *mine,
        places=(spot,),
    )

    def score(arrays, spectra, state, strip, last, micros):
        count = size(arrays)
        shapes = (strip_shape,) * (1 if last else 2)
        scratch = [score_scratch(count)]
        if not spectra:
            shapes += (spectra_shape(count),)
            scratch = [halves_scratch(count)] + scratch
        out = call(
            functools.partial(strip_kernel, len(arrays), len(spectra), len(state), strip),
            "score_strip",
            micros,
            shapes,
            scratch,
            spec,
            tab,
            *state,
            *arrays,
            *spectra,
        )
        return (out, spectra) if spectra else (out[:-1], [out[-1]])

    def chunks(arrays):
        groups = []
        for x in arrays:
            if not groups or size(groups[-1]) + size([x]) > CHUNK:
                groups.append([])
            groups[-1].append(x)
        return groups

    done = [(mine, [own_spectra])]
    early, state = lax.optimization_barrier((early, state))
    for group in chunks(early):
        state, spectra = score(group, [], state, 0, False, EARLY)
        done.append((group, spectra))
    relayed, state = lax.optimization_barrier((relayed, state))
    groups = chunks(relayed) + (chunks([swap(x, "tile") for x in relayed]) if tile_pairs else [])
    for i, group in enumerate(groups):
        state, spectra = score(group, [], state, 0, i == len(groups) - 1, REST)
        done.append((group, spectra))
    log_maps = [state[0]]
    swapped = [swap(state[0], "orient")] if orient_pairs else []
    if sum(size(arrays) for arrays, _ in done) <= CHUNK:
        done = [([x for arrays, _ in done for x in arrays], [x for _, spectra in done for x in spectra])]
    for strip in range(1, n_strip):
        state = ()
        for i, (arrays, spectra) in enumerate(done):
            state, _ = score(arrays, spectra, state, strip, i == len(done) - 1, LAST)
        log_maps.append(state[0])
        if orient_pairs:
            swapped.append(swap(state[0], "orient"))
    pixels = call(functools.partial(pixel_kernel, side), "open_pixels", 1, plane, [], ice_mask)
    stat_shape = jax.ShapeDtypeStruct((8 * (-(-3 * n_strip // 8)), LANES), F32)
    stat, strips = (), []
    for strip, maps in enumerate(zip(log_maps, swapped) if orient_pairs else zip(log_maps)):
        joined, *stat = call(
            functools.partial(join_kernel, len(maps), strip),
            "join_maps",
            COST,
            (strip_shape, stat_shape),
            [],
            *maps,
            pixels,
            *stat,
        )
        strips.append(joined)
    stat = stat[0]
    share = tile // n_orient
    part = jax.ShapeDtypeStruct((share, tile), F32)
    part, opened = call(
        functools.partial(own_rows_kernel, n_strip),
        "own_rows",
        1,
        (part, part),
        [pltpu.VMEM((tile, tile), F32)],
        *strips,
        pixels,
        places=(place,),
    )
    stats = [stat] + [peer(stat, "tile", k) for k in range(1, n_tile)]
    return call(
        functools.partial(norm_kernel, n_strip),
        "normalise",
        1,
        jax.ShapeDtypeStruct((share, tile), F32),
        [],
        part,
        opened,
        *stats,
    )


def solution(mesh):
    return jax.shard_map(
        body,
        mesh=mesh,
        in_specs=(
            P("group", "tile"),
            P("orient", "tile", None, None),
            P("orient", "tile"),
            P(),
            P("group", "tile"),
        ),
        out_specs=P(("group", "orient"), "tile"),
        check_vma=False,
    )
```

```python
import functools
import math

import jax
import jax.numpy as jnp
import ml_dtypes
import numpy as np
from jax import lax
from jax.experimental import pallas as pl
from jax.experimental.pallas import tpu as pltpu
from jax.sharding import PartitionSpec as P

GUARD = 64
MBLK = 16
LANES = 128
PACK = 8
CHUNK = 8
COST = 0.1
OWN, EARLY, REST, LAST = 1, 0.2, 0.4, 2

F32 = jnp.float32
BF16 = jnp.bfloat16
VMEM = pl.BlockSpec(memory_space=pltpu.VMEM)
SMEM = pl.BlockSpec(memory_space=pltpu.SMEM)


def params(mib):
    return pltpu.CompilerParams(vmem_limit_bytes=mib * 2**20)


def high_low(table):
    high = table.astype(np.float32).astype(ml_dtypes.bfloat16)
    low = (table - high.astype(np.float64)).astype(np.float32).astype(ml_dtypes.bfloat16)
    return high, low


def tables(side):
    span = 2 * side
    turn = 2.0 * math.pi * (np.arange(side) + 0.5) / span
    angles = np.outer(np.arange(span), turn)
    high, low = high_low(np.concatenate([np.cos(angles), np.sin(angles)], axis=1))
    middle = np.outer(np.arange(span) - (side - 1) / 2, turn)
    middle_high, middle_low = high_low(np.concatenate([np.cos(middle), np.sin(middle)], axis=1).T)
    away = np.outer(np.arange(side // 2) + 0.5, turn)
    ends = []
    for wave in (np.cos(away), np.sin(away)):
        wave_high, wave_low = high_low(wave)
        ends += [np.concatenate([wave_high, wave_high], axis=1), np.concatenate([wave_low, wave_low], axis=1)]
    return np.concatenate([high, low, high.T, low.T, *ends, middle_high, middle_low], axis=0)


def tall(tab_ref, count):
    span = tab_ref.shape[1]
    high, low = tab_ref[0:count, :], tab_ref[span : span + count, :]
    return jnp.concatenate([high, high, low], axis=0)


def wide(high, low):
    return jnp.concatenate([high, high, low], axis=1)


def back_cols(tab_ref, side):
    span = tab_ref.shape[1]
    both = jnp.concatenate([tab_ref[2 * span : 3 * span, 0:side], tab_ref[3 * span : 4 * span, 0:side]], axis=1)
    return jnp.concatenate([both, both], axis=0)


def split(x):
    high = x.astype(BF16)
    return high, (x - high.astype(F32)).astype(BF16)


def tripled(x, axis):
    high, low = split(x)
    return jnp.concatenate([high, low, high], axis=axis)


def doubled(x, axis):
    return jnp.concatenate(split(x), axis=axis)


def halves(x, axis):
    half = x.shape[axis] // 2
    return x[:half] + x[half:] if axis == 0 else x[:, :half] + x[:, half:]


def product(left, right):
    return jnp.dot(left, right, preferred_element_type=F32)


def paired(quads, side):
    cc, cs = quads[:side, :side], quads[:side, side:]
    sc, ss = quads[side:, :side], quads[side:, side:]
    return cc - ss, sc + cs, cc + ss, sc - cs


def image_spectra(spot_ref, inner_ref, own_ref, outer_ref, tab_ref, spec_ref):
    odd = spot_ref[0] % 2 == 1

    def edge(ref):
        lines = ref[...]
        return jnp.concatenate([lines[:, :GUARD], lines[:, GUARD:]], axis=0)

    inner, outer = edge(inner_ref), edge(outer_ref)
    left, right = jnp.where(odd, inner, outer), jnp.where(odd, outer, inner)
    image = jnp.concatenate([left, own_ref[...], right], axis=1)
    side = spec_ref.shape[-1]
    span = 2 * side
    rows, cols = image.shape[0] // side - 1, image.shape[1] // side - 1
    scale = 2.0 / (span * span)
    cols_table, rows_table = tall(tab_ref, span), wide(tab_ref[5 * span : 6 * span, :], tab_ref[6 * span :, :])
    for q in range(cols):
        half = product(tripled(image[:, q * side : q * side + span], 1), cols_table)
        for p in range(rows):
            full = product(rows_table, tripled(half[p * side : p * side + span], 0))
            for part, value in enumerate(paired(full, side)):
                spec_ref[p * cols + q, part] = value * scale


def transform(patches, tab_ref, half_ref, patch_ref):
    side = patch_ref.shape[-1]
    span = 2 * side
    patch_cols = tall(tab_ref, side)
    patch_rows = wide(tab_ref[2 * span : 3 * span, 0:side], tab_ref[3 * span : 4 * span, 0:side])
    for first in range(0, len(patches), 4):
        group = patches[first : first + 4]
        half = product(tripled(jnp.concatenate(group, axis=0), 1), patch_cols)
        for i in range(len(group)):
            high, low = split(half[i * side : (i + 1) * side])
            half_ref[first + i, 0:side] = high
            half_ref[first + i, side : 2 * side] = low
            half_ref[first + i, 2 * side : 3 * side] = high

    def finish(n, carry):
        for part, value in enumerate(paired(product(patch_rows, half_ref[n]), side)):
            patch_ref[n, part] = value
        return carry

    lax.fori_loop(0, len(patches), finish, 0, unroll=steps_at_once(len(patches), 8))


def steps_at_once(count, most):
    return max(u for u in range(1, most + 1) if count % u == 0)


def correlate(spec_ref, tab_ref, patch_refs, strip, score_ref):
    side = spec_ref.shape[-1]
    span = 2 * side
    cols = score_ref.shape[2] // side
    even_rows, odd_rows = tab_ref[4 * span : 4 * span + side, :], tab_ref[4 * span + side : 5 * span, :]
    cols_table = back_cols(tab_ref, side)
    first = 0
    for patch_ref in patch_refs:

        def score(n, carry, patch_ref=patch_ref, first=first):
            tr, tu, sr, si = (patch_ref[n, part] for part in range(4))
            for q in range(cols):
                ir, iu, jr, ji = (spec_ref[strip * cols + q, part] for part in range(4))
                a, b = ir * tr + iu * tu, iu * tr - ir * tu
                c, e = jr * sr + ji * si, jr * si - ji * sr
                top = jnp.concatenate([a + c, e + b], axis=1)
                low = jnp.concatenate([b - e, c - a], axis=1)
                even = halves(product(even_rows, doubled(top, 0)), 0)
                odd = halves(product(odd_rows, doubled(low, 0)), 0)
                lines = jnp.concatenate([even + odd, even - odd], axis=0)
                score_ref[first + n, :, q * side : (q + 1) * side] = halves(product(doubled(lines, 1), cols_table), 1)
            return carry

        count = patch_ref.shape[0]
        lax.fori_loop(0, count, score, 0, unroll=steps_at_once(count, 16 // cols))
        first += count


STRIP = 64


def fold(score_ref, weights, state, out):
    def strip(r, carry):
        rows = pl.ds(pl.multiple_of(r * STRIP, STRIP), STRIP)
        values = [score_ref[n, rows, :] + weight for n, weight in enumerate(weights)]
        top = values[0]
        for value in values[1:]:
            top = jnp.maximum(top, value)
        if state:
            old_top, old_sum = state[0][rows, :], state[1][rows, :]
            top = jnp.maximum(top, old_top)
        total = jnp.exp(values[0] - top)
        for value in values[1:]:
            total = total + jnp.exp(value - top)
        if state:
            total = total + old_sum * jnp.exp(old_top - top)
        if len(out) == 1:
            out[0][rows, :] = top + jnp.log(total)
        else:
            out[0][rows, :] = top
            out[1][rows, :] = total
        return carry

    lax.fori_loop(0, score_ref.shape[1] // STRIP, strip, 0, unroll=True)


def unpack(refs, side):
    patches, weights = [], []
    for ref in refs:
        places = [()] if len(ref.shape) == 2 else [(i,) for i in range(ref.shape[0])]
        for place in places:
            patches.append(ref[place + (slice(0, side), slice(None))])
            weights.append(ref[place + (slice(side, side + 1), slice(0, 1))])
    return patches, weights


def own_kernel(n_in, strip, *refs):
    tab_ref, packs = refs[4], refs[5 : 5 + n_in]
    spec_ref, *out, patch_ref, half_ref, score_ref = refs[5 + n_in :]
    image_spectra(*refs[:5], spec_ref)
    patches, weights = unpack(packs, spec_ref.shape[-1])
    transform(patches, tab_ref, half_ref, patch_ref)
    correlate(spec_ref, tab_ref, [patch_ref], strip, score_ref)
    fold(score_ref, weights, (), out)


def strip_kernel(n_in, n_spectra, n_state, strip, *refs):
    spec_ref, tab_ref, refs = refs[0], refs[1], refs[2:]
    state, packs, refs = refs[:n_state], refs[n_state : n_state + n_in], refs[n_state + n_in :]
    patches, weights = unpack(packs, spec_ref.shape[-1])
    if n_spectra:
        patch_refs, (*out, score_ref) = refs[:n_spectra], refs[n_spectra:]
    else:
        *out, patch_ref, half_ref, score_ref = refs
        transform(patches, tab_ref, half_ref, patch_ref)
        patch_refs = [patch_ref]
    correlate(spec_ref, tab_ref, patch_refs, strip, score_ref)
    fold(score_ref, weights, state, out)


def folded(stored, side):
    within = stored % side
    return stored - within + jnp.where(within < side // 2, within + side // 2, side - 1 - within)


def keeper(row, side):
    within = row % side
    return row - within + jnp.where(within < side // 2, side - 1 - within, within - side // 2)


def pixel_kernel(side, mask_ref, pixel_ref):
    blocks = (1.0 - mask_ref[...].astype(F32)).astype(BF16)
    rows, cols = blocks.shape
    pixel = folded(lax.broadcasted_iota(jnp.int32, (rows * MBLK, rows), 0), side)
    block = lax.broadcasted_iota(jnp.int32, (rows * MBLK, rows), 1)
    down = (pixel // MBLK == block).astype(F32).astype(BF16)
    pixel = lax.broadcasted_iota(jnp.int32, (cols, cols * MBLK), 1)
    block = lax.broadcasted_iota(jnp.int32, (cols, cols * MBLK), 0)
    across = (pixel // MBLK == block).astype(F32).astype(BF16)
    pixel_ref[...] = product(product(down, blocks).astype(BF16), across)


def join_kernel(n_map, strip, *refs):
    maps, (pixel_ref, *before, log_ref, stat_ref) = refs[:n_map], refs[n_map:]
    values = maps[0][...]
    for ref in maps[1:]:
        other = ref[...]
        top = jnp.maximum(values, other)
        values = top + jnp.log(1.0 + jnp.exp(jnp.minimum(values, other) - top))
    log_ref[...] = values
    side = values.shape[0]
    pixels = pixel_ref[strip * side : (strip + 1) * side, :]
    count = jnp.sum(pixels)
    total = jnp.sum(pixels * values)
    deviation = values - total / jnp.maximum(count, 1.0)
    squares = jnp.sum(pixels * deviation * deviation)
    row = lax.broadcasted_iota(jnp.int32, stat_ref.shape, 0)
    stat = before[0][...] if before else jnp.zeros(stat_ref.shape, F32)
    for i, value in enumerate((count, total, squares)):
        stat = jnp.where(row == 3 * strip + i, value, stat)
    stat_ref[...] = stat


def own_rows_kernel(n_strip, place_ref, *refs):
    strips, (pixel_ref, part_ref, open_ref, log_ref) = refs[:n_strip], refs[n_strip:]
    side = strips[0].shape[0]
    share = part_ref.shape[0]
    for i, ref in enumerate(strips):
        log_ref[i * side : (i + 1) * side, :] = ref[...]

    def unfold(i, carry):
        row = keeper(place_ref[0] * share + i, side)
        part_ref[pl.ds(i, 1), :] = log_ref[pl.ds(row, 1), :]
        open_ref[pl.ds(i, 1), :] = pixel_ref[pl.ds(row, 1), :]
        return carry

    lax.fori_loop(0, share, unfold, 0, unroll=8)


def norm_kernel(n_strip, part_ref, open_ref, *refs):
    stats, out_ref = refs[:-1], refs[-1]
    rows = [(ref[...], 3 * strip) for ref in stats for strip in range(n_strip)]
    counts = [stat[i : i + 1] for stat, i in rows]
    totals = [stat[i + 1 : i + 2] for stat, i in rows]
    count, total = sum(counts), sum(totals)
    average = total / count
    squares = 0.0
    for (stat, i), n, s in zip(rows, counts, totals):
        apart = s / jnp.maximum(n, 1.0) - average
        squares = squares + stat[i + 2 : i + 3] + n * apart * apart
    scale = 1.0 / jnp.sqrt(squares / count + 1e-05)
    for i in range(0, out_ref.shape[1], LANES):
        cols = slice(i, i + LANES)
        out_ref[:, cols] = open_ref[:, cols] * (part_ref[:, cols] - average) * scale


def shift(i, step, n):
    return i ^ step if n & (n - 1) == 0 else (i + step) % n


def peer(x, axis, step):
    n = lax.axis_size(axis)
    return lax.ppermute(x, axis, [(i, shift(i, step, n)) for i in range(n)])


def swap(x, axis):
    return lax.ppermute(x, axis, [(i, i ^ 1) for i in range(lax.axis_size(axis))])


def exchange(x, axis, start):
    pairs = [(i, i + 1) for i in range(start, lax.axis_size(axis) - 1, 2)]
    return lax.ppermute(x, axis, pairs + [(j, i) for i, j in pairs]) if pairs else jnp.zeros_like(x)


def pack_kernel(ids_ref, weight_ref, patch_ref, pack_ref, weights, sems):
    side = patch_ref.shape[0]
    pairs = ((patch_ref, pack_ref.at[0:side]), (weight_ref, weights))
    copies = [pltpu.make_async_copy(source, target, sems.at[i]) for i, (source, target) in enumerate(pairs)]
    for copy in copies:
        copy.start()
    for copy in copies:
        copy.wait()
    catalog = lax.broadcasted_iota(jnp.int32, weights.shape, 1)
    weight = jnp.sum(jnp.where(catalog == ids_ref[0, 0], weights[...], 0.0), axis=1, keepdims=True)
    pack_ref[side:, :] = jnp.broadcast_to(weight, (PACK, side))


def edge_kernel(spot_ref, own_ref, tab_ref, inner_ref, outer_ref):
    half = own_ref.shape[0] // 2
    own = own_ref[...]
    edges = [own[:, :GUARD], own[:, own.shape[1] - GUARD :]]
    left, right = [jnp.concatenate([x[:half], x[half:]], axis=1) for x in edges]
    odd = spot_ref[0] % 2 == 1
    inner_ref[...] = jnp.where(odd, left, right)
    outer_ref[...] = jnp.where(odd, right, left)


def stack_kernel(*refs):
    for i, ref in enumerate(refs[:-1]):
        refs[-1][i] = ref[...]


def cost(micros):
    return pl.CostEstimate(flops=int(micros * 1e9), bytes_accessed=0, transcendentals=0)


def body(micrograph, templates, orient_ids, log_weight, ice_mask):
    side = templates.shape[2]
    tile = micrograph.shape[1]
    blocks = (tile // side) ** 2
    tab = jnp.asarray(tables(side))
    n_tile, n_orient = lax.axis_size("tile"), lax.axis_size("orient")
    place = lax.axis_index("orient").astype(jnp.int32).reshape(1)
    spot = lax.axis_index("tile").astype(jnp.int32).reshape(1)
    stay = [pltpu.with_memory_space_constraint(x, pltpu.HBM) for x in (log_weight.reshape(1, -1), templates.reshape(side, side))]
    pack = pl.pallas_call(
        pack_kernel,
        out_shape=jax.ShapeDtypeStruct((side + PACK, side), F32),
        in_specs=[SMEM, pl.BlockSpec(memory_space=pltpu.HBM), pl.BlockSpec(memory_space=pltpu.HBM)],
        out_specs=VMEM,
        scratch_shapes=[pltpu.VMEM((1, log_weight.shape[0]), F32), pltpu.SemaphoreType.DMA((2,))],
        compiler_params=params(4),
        cost_estimate=cost(1),
        name="pack_weight",
    )(orient_ids, *stay)
    micrograph, pack = lax.optimization_barrier((micrograph, pack))
    edge = jax.ShapeDtypeStruct((micrograph.shape[0] // 2, 2 * GUARD), F32)
    inner_edge, outer_edge = pl.pallas_call(
        edge_kernel,
        out_shape=(edge, edge),
        in_specs=[SMEM, VMEM, VMEM],
        out_specs=(VMEM, VMEM),
        compiler_params=params(4),
        cost_estimate=cost(0.5),
        name="edges",
    )(spot, micrograph, tab)

    tile_pairs, orient_pairs = n_tile % 2 == 0, n_orient % 2 == 0
    tile_steps = range(0, n_tile, 2 if tile_pairs else 1)
    orient_steps = range(0, n_orient, 2 if orient_pairs else 1)
    far = [peer(pack, "orient", o) for o in orient_steps[1:]]
    inner, outer = exchange(inner_edge, "tile", 0), exchange(outer_edge, "tile", 1)
    mine = [pack] + ([swap(pack, "tile")] if tile_pairs else [])

    plane = jax.ShapeDtypeStruct((tile, tile), F32)

    strip_shape = jax.ShapeDtypeStruct((side, tile), F32)
    half_shape, patch_shape = (3 * side, 2 * side), (4, side, side)

    def size(arrays):
        return sum(x.shape[0] if x.ndim == 3 else 1 for x in arrays)

    def call(kernel, name, micros, shapes, scratch, *operands, places=(), mib=24):
        return pl.pallas_call(
            kernel,
            out_shape=shapes,
            in_specs=[SMEM] * len(places) + [VMEM] * len(operands),
            out_specs=jax.tree.map(lambda _: VMEM, shapes),
            scratch_shapes=scratch,
            compiler_params=params(mib),
            cost_estimate=cost(micros),
            name=name,
        )(*places, *operands)

    def spectra_shape(count):
        return jax.ShapeDtypeStruct((count, *patch_shape), F32)

    def halves_scratch(count):
        return pltpu.VMEM((count, *half_shape), BF16)

    def score_scratch(count):
        return pltpu.VMEM((count, side, tile), F32)

    n_strip = tile // side
    held = call(stack_kernel, "stack_packs", COST, jax.ShapeDtypeStruct((1 + len(far), *pack.shape), F32), [], pack, *far)
    relayed = [peer(held, "tile", t) for t in tile_steps[1:]]
    early = far + ([swap(x, "tile") for x in far] if tile_pairs else [])
    spec, *state, own_spectra = call(
        functools.partial(own_kernel, len(mine), 0),
        "own_block",
        OWN,
        (jax.ShapeDtypeStruct((blocks, 4, side, side), F32), strip_shape, strip_shape, spectra_shape(len(mine))),
        [halves_scratch(len(mine)), score_scratch(len(mine))],
        inner,
        micrograph,
        outer,
        tab,
        *mine,
        places=(spot,),
    )

    def score(arrays, spectra, state, strip, last, micros):
        count = size(arrays)
        shapes = (strip_shape,) * (1 if last else 2)
        scratch = [score_scratch(count)]
        if not spectra:
            shapes += (spectra_shape(count),)
            scratch = [halves_scratch(count)] + scratch
        out = call(
            functools.partial(strip_kernel, len(arrays), len(spectra), len(state), strip),
            "score_strip",
            micros,
            shapes,
            scratch,
            spec,
            tab,
            *state,
            *arrays,
            *spectra,
        )
        return (out, spectra) if spectra else (out[:-1], [out[-1]])

    def chunks(arrays):
        groups = []
        for x in arrays:
            if not groups or size(groups[-1]) + size([x]) > CHUNK:
                groups.append([])
            groups[-1].append(x)
        return groups

    done = [(mine, [own_spectra])]
    early, state = lax.optimization_barrier((early, state))
    for group in chunks(early):
        state, spectra = score(group, [], state, 0, False, EARLY)
        done.append((group, spectra))
    relayed, state = lax.optimization_barrier((relayed, state))
    groups = chunks(relayed) + (chunks([swap(x, "tile") for x in relayed]) if tile_pairs else [])
    for i, group in enumerate(groups):
        state, spectra = score(group, [], state, 0, i == len(groups) - 1, REST)
        done.append((group, spectra))
    log_maps = [state[0] if groups else state[0] + jnp.log(state[1])]
    swapped = [swap(log_maps[0], "orient")] if orient_pairs else []
    if sum(size(arrays) for arrays, _ in done) <= CHUNK:
        done = [([x for arrays, _ in done for x in arrays], [x for _, spectra in done for x in spectra])]
    for strip in range(1, n_strip):
        state = ()
        for i, (arrays, spectra) in enumerate(done):
            state, _ = score(arrays, spectra, state, strip, i == len(done) - 1, LAST)
        log_maps.append(state[0])
        if orient_pairs:
            swapped.append(swap(state[0], "orient"))
    pixels = call(functools.partial(pixel_kernel, side), "open_pixels", 1, plane, [], ice_mask)
    stat_shape = jax.ShapeDtypeStruct((8 * (-(-3 * n_strip // 8)), LANES), F32)
    stat, strips = (), []
    for strip, maps in enumerate(zip(log_maps, swapped) if orient_pairs else zip(log_maps)):
        joined, *stat = call(
            functools.partial(join_kernel, len(maps), strip),
            "join_maps",
            COST,
            (strip_shape, stat_shape),
            [],
            *maps,
            pixels,
            *stat,
        )
        strips.append(joined)
    stat = stat[0]
    share = tile // n_orient
    part = jax.ShapeDtypeStruct((share, tile), F32)
    part, opened = call(
        functools.partial(own_rows_kernel, n_strip),
        "own_rows",
        1,
        (part, part),
        [pltpu.VMEM((tile, tile), F32)],
        *strips,
        pixels,
        places=(place,),
    )
    stats = [stat] + [peer(stat, "tile", k) for k in range(1, n_tile)]
    return call(
        functools.partial(norm_kernel, n_strip),
        "normalise",
        1,
        jax.ShapeDtypeStruct((share, tile), F32),
        [],
        part,
        opened,
        *stats,
    )


def solution(mesh):
    return jax.shard_map(
        body,
        mesh=mesh,
        in_specs=(
            P("group", "tile"),
            P("orient", "tile", None, None),
            P("orient", "tile"),
            P(),
            P("group", "tile"),
        ),
        out_specs=P(("group", "orient"), "tile"),
        check_vma=False,
    )
```
